32 devices in a mesh: wide: 8 (over y, x, core), narrow: 4 (over z).
Axes of the slice: x: 2, y: 2, z: 4, core: 2. Of those that a mesh axis runs over, the one named last changes fastest.
Arguments:
- user_input: bfloat16 [64, 64, 2048], P('wide'), may hold values from -6 to 6
- out_grad: bfloat16 [64, 64, 2048], P('wide'), may hold values from -6 to 6
- hist_len: int32 [64], P('wide'), may hold values from 1 to 64, 3072 in all
- hist_items: int32 [64, 64], P('wide'), may hold values from 0 to 1023, as said below
- item_row: int32 [1024], replicated, may hold values from 0 to 1023, as said below
- item_feat: bfloat16 [1024, 2048], P('wide'), may hold values from -6 to 6
- user_gain: bfloat16 [2048], replicated, may hold values from 0.5 to 1.5
- user_gate: bfloat16 [2048, 3072], P(None, 'narrow'), may hold values from -0.125 to 0.125
- user_up: bfloat16 [2048, 3072], P(None, 'narrow'), may hold values from -0.125 to 0.125
- user_down: bfloat16 [3072, 2048], P('narrow'), may hold values from -0.109375 to 0.109375
- item_gain: bfloat16 [2048], replicated, may hold values from 0.5 to 1.5
- item_gate: bfloat16 [2048, 3072], P(None, 'narrow'), may hold values from -0.125 to 0.125
- item_up: bfloat16 [2048, 3072], P(None, 'narrow'), may hold values from -0.125 to 0.125
- item_down: bfloat16 [3072, 2048], P('narrow'), may hold values from -0.109375 to 0.109375
Outputs:
- item_feat_grad: bfloat16 [1024, 2048], P('wide')
- user_gate_grad: float32 [2048, 3072], P('wide', 'narrow')
- user_up_grad: float32 [2048, 3072], P('wide', 'narrow')
- user_down_grad: float32 [3072, 2048], P('narrow', 'wide')
- item_gate_grad: float32 [2048, 3072], P('wide', 'narrow')
- item_up_grad: float32 [2048, 3072], P('wide', 'narrow')
- item_down_grad: float32 [3072, 2048], P('narrow', 'wide')
The draws below stay inside these ranges and needn't reach their ends.
Inputs may be any that keep to these rules, and one draw needn't show every extreme that they name: `hist_items`: among the 512 positions of one index of wide, at most 128 name items whose table rows lie on any one index of wide; the rows of one index of wide, the same for all, are named by exactly 128 positions of every index of wide. A permutation: item id i lies in table row item_row[i], held by index item_row[i] // 128 of wide.
All inputs are finite; a program needn't handle non-finite values. No bound on the sum of `hist_len` on one device may be relied on, other than what follows from the above.
Results may differ from the reference program's by a relative error of at most 0.027.
Values may be sent and summed in bfloat16 or wider, within the bound.
No kernel may reach another device: no remote copies, remote signals or barrier semaphores. Data moves between devices by JAX's collectives and lax.ppermute only.
A program may use at most 128 MiB of HBM per device.

```python
import math
import jax
import jax.numpy as jnp
import numpy as np
from jax import lax

D = 2048
HID = 3072
LEN = 64
ITEM_DEV = 128
HIST_ROWS = 512
USERS = 64
ITEMS = 1024
CAP = 128
N_WIDE = 8


def table_order(key):
    return jax.random.permutation(jax.random.fold_in(key, 11), ITEMS).astype(jnp.int32)


def draw_item_row(key, part):
    return table_order(key)


def draw_hist_items(key, part):
    order = table_order(key)
    inverse = jnp.argsort(order).astype(jnp.int32)
    key = jax.random.fold_in(key, 3)
    hot_owner = jax.random.randint(jax.random.fold_in(key, 1), (), 0, N_WIDE).astype(jnp.int32)
    block_keys = jax.random.split(jax.random.fold_in(key, 2), N_WIDE)

    def one_block(block_key):
        first_key, second_key, third_key = jax.random.split(block_key, 3)
        picks = jax.random.permutation(first_key, (N_WIDE - 1) * CAP)[:HIST_ROWS - CAP].astype(jnp.int32)
        others = picks // CAP
        others = others + (others >= hot_owner).astype(jnp.int32)
        owners = jnp.concatenate([jnp.full((CAP,), hot_owner, jnp.int32), others])
        owners = owners[jax.random.permutation(second_key, HIST_ROWS)]
        local_rows = jax.random.randint(third_key, (HIST_ROWS,), 0, ITEM_DEV).astype(jnp.int32)
        return inverse[owners * ITEM_DEV + local_rows]
    return jax.vmap(one_block)(block_keys).reshape(USERS, LEN).astype(jnp.int32)


def shard_levels(rng, extent, shards, low, largest):
    gain, own = 1.0, jax.random.fold_in(rng, 6)
    for position, shards_of in shards:
        heights = jnp.exp(jax.random.uniform(jax.random.fold_in(own, position), (shards_of,), jnp.float32, low / len(shards), largest / len(shards)))
        gain = gain * jnp.repeat(heights, extent[position] // shards_of).reshape([-1 if axis == position else 1 for axis in range(len(extent))])
    return gain


def profile(number_of, total, reach, lean):
    weights = [(1 << 20) // math.isqrt(standing ** lean) + 1 for standing in range(2, number_of + 1)]
    spare, holding = total - reach - (number_of - 1), [1] * (number_of - 1)
    while spare > 0:
        candidates = [i for i in range(number_of - 1) if holding[i] < reach]
        mass, remaining = sum([weights[i] for i in candidates]), spare
        for i in candidates:
            addition = min(reach - holding[i], max(1, remaining * weights[i] // mass), spare)
            holding[i] = holding[i] + addition
            spare = spare - addition
    return np.array([reach] + holding)


def uneven_parts(key, count, total, limit, skew):
    if count == 2:
        one = jax.random.randint(key, (), max(1, total - limit), min(limit, total - 1) + 1)
        return jnp.stack([one, total - one])
    tallies = jnp.asarray(profile(count, total, limit, skew), jnp.int32)
    pairs = (count - 1) // 2
    source_of, taker = tallies[1:1 + 2 * pairs:2], tallies[2:2 + 2 * pairs:2]
    room = jnp.minimum(source_of - 1, limit - taker)
    passed = jax.random.randint(jax.random.fold_in(key, 1), (pairs,), 0, 1 << 20) % (room + 1)
    tallies = tallies.at[1:1 + 2 * pairs:2].set(source_of - passed).at[2:2 + 2 * pairs:2].set(taker + passed)
    return tallies[jax.random.permutation(jax.random.fold_in(key, 2), count)]


def normal_values(key, shape, width, reach, cuts=(), kind=jnp.bfloat16):
    values = jax.random.normal(key, shape, jnp.float32) * width
    if len(cuts) > 0:
        values = shard_levels(key, shape, cuts, -0.22, 0.18) * values
    return jnp.clip(values, min=-reach, max=reach).astype(kind)


def setup_inputs(seed: int = 0) -> dict:
    seeds = jax.random.split(jax.random.key(seed), 15)
    user_input = normal_values(seeds[0], (USERS, LEN, D), 1.0, 6.0, ((0, 8),))
    out_grad = normal_values(seeds[1], (USERS, LEN, D), 1.0, 6.0, ((0, 8),))
    hist_len = uneven_parts(seeds[2], USERS, USERS * LEN * 3 // 4, LEN, 1).astype(jnp.int32)
    hist_items = draw_hist_items(jax.random.fold_in(seeds[14], 71), 0)
    item_row = draw_item_row(jax.random.fold_in(seeds[14], 71), 0)
    item_feat = normal_values(seeds[5], (ITEMS, D), 1.0, 6.0, ((0, 8),))
    user_gain = jnp.clip(1.0 + 0.1 * jax.random.normal(seeds[6], (D,), jnp.float32), 0.5, 1.5).astype(jnp.bfloat16)
    user_gate = normal_values(seeds[7], (D, HID), D ** -0.5, 0.125, ((1, 4),))
    user_up = normal_values(seeds[8], (D, HID), D ** -0.5, 0.125, ((1, 4),))
    user_down = normal_values(seeds[9], (HID, D), HID ** -0.5, 0.109375, ((0, 4),))
    item_gain = jnp.clip(1.0 + 0.1 * jax.random.normal(seeds[10], (D,), jnp.float32), 0.5, 1.5).astype(jnp.bfloat16)
    item_gate = normal_values(seeds[11], (D, HID), D ** -0.5, 0.125, ((1, 4),))
    item_up = normal_values(seeds[12], (D, HID), D ** -0.5, 0.125, ((1, 4),))
    item_down = normal_values(seeds[13], (HID, D), HID ** -0.5, 0.109375, ((0, 4),))
    return dict(user_input=user_input, out_grad=out_grad, hist_len=hist_len, hist_items=hist_items, item_row=item_row, item_feat=item_feat, user_gain=user_gain, user_gate=user_gate, user_up=user_up, user_down=user_down, item_gain=item_gain, item_gate=item_gate, item_up=item_up, item_down=item_down)


def layer_back(row_vals, gain_vec, w_gate, w_up, w_down, cot_rows):
    floats = row_vals.astype(jnp.float32)
    inv_rms = lax.rsqrt(lax.optimization_barrier(jnp.mean(floats * floats, axis=1, keepdims=True)) + 1e-05)
    unit_rows = floats * inv_rms
    gain_f = gain_vec.astype(jnp.float32)
    normed = (unit_rows * gain_f).astype(jnp.bfloat16)
    gate_act = jnp.dot(normed, w_gate, preferred_element_type=jnp.float32)
    up_act = jnp.dot(normed, w_up, preferred_element_type=jnp.float32)
    sig_gate = jax.nn.sigmoid(gate_act)
    hidden = (gate_act * sig_gate * up_act).astype(jnp.bfloat16)
    cot_bf = cot_rows.astype(jnp.bfloat16)
    d_hidden = jnp.dot(cot_bf, w_down.T, preferred_element_type=jnp.float32)
    d_up = (d_hidden * gate_act * sig_gate).astype(jnp.bfloat16)
    d_gate = (d_hidden * up_act * sig_gate * (1.0 + gate_act * (1.0 - sig_gate))).astype(jnp.bfloat16)
    d_normed = jnp.dot(d_gate, w_gate.T, preferred_element_type=jnp.float32) + jnp.dot(d_up, w_up.T, preferred_element_type=jnp.float32)
    scaled = gain_f * d_normed
    row_mean = lax.optimization_barrier(jnp.mean(scaled * unit_rows, axis=1, keepdims=True))
    d_rows = cot_rows + inv_rms * (scaled - unit_rows * row_mean)
    return (d_rows, normed, hidden, cot_bf, d_gate, d_up)

def replica_mean(normed, hidden, cot_bf, d_gate, d_up):
    model_width = normed.shape[1]
    hidden_width = hidden.shape[1]

    def add_block(carry, block):
        normed_b, hidden_b, cot_b, gate_b, up_b = block
        terms = (jnp.dot(normed_b.T, gate_b, preferred_element_type=jnp.float32), jnp.dot(normed_b.T, up_b, preferred_element_type=jnp.float32), jnp.dot(hidden_b.T, cot_b, preferred_element_type=jnp.float32))
        rounded = tuple((lax.optimization_barrier(term.astype(jnp.bfloat16)).astype(jnp.float32) for term in terms))
        return (tuple((total + piece for total, piece in zip(carry, rounded))), None)

    def blocked(array):
        return array.reshape(N_WIDE, array.shape[0] // N_WIDE, array.shape[1])
    start_sums = (jnp.zeros((model_width, hidden_width), jnp.float32), jnp.zeros((model_width, hidden_width), jnp.float32), jnp.zeros((hidden_width, model_width), jnp.float32))
    totals = lax.scan(add_block, start_sums, tuple((blocked(array) for array in (normed, hidden, cot_bf, d_gate, d_up))))[0]
    return tuple((total / N_WIDE for total in totals))

def reference(user_input, out_grad, hist_len, hist_items, item_row, item_feat, user_gain, user_gate, user_up, user_down, item_gain, item_gate, item_up, item_down):
    valid = (jnp.arange(LEN, dtype=jnp.int32)[None, :] < hist_len[:, None]).astype(jnp.float32)
    masked = (out_grad.astype(jnp.float32) * valid[:, :, None]).astype(jnp.bfloat16).reshape(USERS * LEN, D)
    user_rows = user_input.reshape(USERS * LEN, D)
    occ_grad, normed, hidden, cot_bf, d_gate, d_up = layer_back(user_rows, user_gain, user_gate, user_up, user_down, masked.astype(jnp.float32))
    user_grads = replica_mean(normed, hidden, cot_bf, d_gate, d_up)
    targets = item_row[hist_items.reshape(USERS * LEN)].astype(jnp.int32)
    item_in = jax.ops.segment_sum(occ_grad, targets, num_segments=ITEMS)
    item_rows, normed_i, hidden_i, cot_i, gate_i, up_i = layer_back(item_feat, item_gain, item_gate, item_up, item_down, item_in)
    item_grads = replica_mean(normed_i, hidden_i, cot_i, gate_i, up_i)
    return (item_rows.astype(jnp.bfloat16), user_grads[0], user_grads[1], user_grads[2], item_grads[0], item_grads[1], item_grads[2])
```

```python
import jax
import jax.numpy as jnp
from jax import lax
from jax.sharding import PartitionSpec as P

F32 = jnp.float32
BF16 = jnp.bfloat16
LAST = (((1,), (1,)), ((), ()))
FIRST = (((0,), (0,)), ((), ()))


def mm(a, b, dims=(((1,), (0,)), ((), ()))):
    return lax.dot_general(a, b, dims, preferred_element_type=F32)


def swap(value, axis, bit):
    count = lax.axis_size(axis)
    return lax.ppermute(value, axis, [(i, i ^ bit) for i in range(count)])


def shift(value, axis, step):
    count = lax.axis_size(axis)
    return lax.ppermute(value, axis, [(i, (i + step) % count) for i in range(count)])


def bit_orders(count):
    bits = [1 << k for k in range(1, count.bit_length() - 1)]
    half = len(bits) // 2
    return bits, bits[half:] + bits[:half]


def pick(blocks, bits, bit, value):
    return lax.dynamic_index_in_dim(blocks, value, axis=bits.index(bit), keepdims=False)


def halve(blocks, order, me):
    bits = sorted(order, reverse=True)
    for position, bit in enumerate(order):
        mine = (me // bit) % 2
        sent = pick(blocks, bits, bit, 1 - mine)
        kept = pick(blocks, bits, bit, mine)
        total = kept.astype(F32) + swap(sent, "wide", bit).astype(F32)
        bits.remove(bit)
        blocks = total.astype(BF16) if position < len(order) - 1 else total
    return blocks


def gather(piece, order):
    for bit in order:
        piece = jnp.concatenate([piece, swap(piece, "wide", bit)], axis=0)
    return piece


def offsets(order):
    found = [0]
    for bit in order:
        found = found + [j ^ bit for j in found]
    return found


def norm_parts(row_vals, gain_vec):
    floats = row_vals.astype(F32)
    inv_rms = lax.rsqrt(jnp.mean(floats * floats, axis=1, keepdims=True) + 1e-05)
    unit_rows = floats * inv_rms
    gain_f = gain_vec.astype(F32)
    return unit_rows, inv_rms, gain_f, (unit_rows * gain_f).astype(BF16)


def grads(gate_act, up_act, d_hidden):
    sig = jax.nn.sigmoid(gate_act)
    hidden = (gate_act * sig * up_act).astype(BF16)
    d_up = (d_hidden * gate_act * sig).astype(BF16)
    d_gate = (d_hidden * up_act * sig * (1.0 + gate_act * (1.0 - sig))).astype(BF16)
    return hidden, d_gate, d_up


def body(
    user_input,
    out_grad,
    hist_len,
    hist_items,
    item_row,
    item_feat,
    user_gain,
    user_gate,
    user_up,
    user_down,
    item_gain,
    item_gate,
    item_up,
    item_down,
):
    n_wide, n_narrow = lax.axis_size("wide"), lax.axis_size("narrow")
    me, here = lax.axis_index("wide"), lax.axis_index("narrow")
    core = me % 2
    order_a, order_b = bit_orders(n_wide)
    cubes = (2,) * len(order_a)
    user_count, hist_length, width = user_input.shape
    rows = user_count * hist_length
    item_dev = item_feat.shape[0]
    hid = user_gate.shape[1]
    block = width // n_wide

    item_unit, item_inv, item_gain_f, item_normed = norm_parts(item_feat, item_gain)
    item_gate_act = mm(item_normed, item_gate)
    item_up_act = mm(item_normed, item_up)
    item_hidden = (item_gate_act * jax.nn.sigmoid(item_gate_act) * item_up_act).astype(BF16)
    half = item_dev // 2
    ag_a, ag_b = order_a + [1], order_b + [1]

    def gathered(value):
        return jnp.concatenate([gather(value[:half], ag_a), gather(value[half:], ag_b)], axis=0)

    def columns(value):
        parts = {}
        for j in range(n_wide):
            to = me ^ j
            part = lax.dynamic_slice_in_dim(value, to * block, block, axis=1)
            parts[j] = part if j == 0 else swap(part, "wide", j)
        return jnp.concatenate(
            [parts[j][:half] for j in offsets(ag_a)] + [parts[j][half:] for j in offsets(ag_b)], axis=0
        )

    all_hidden = gathered(item_hidden)
    all_normed = columns(item_normed)

    user_rows = user_input.reshape(rows, width)
    valid = (jnp.arange(hist_length, dtype=jnp.int32)[None, :] < hist_len[:, None]).astype(F32)
    masked = (out_grad.astype(F32) * valid[:, :, None]).astype(BF16).reshape(rows, width)
    unit_rows, inv_rms, gain_f, normed = norm_parts(user_rows, user_gain)
    gate_act = mm(normed, user_gate)
    up_act = mm(normed, user_up)
    d_hidden = mm(masked, user_down, LAST)
    hidden, d_gate, d_up = grads(gate_act, up_act, d_hidden)
    scaled = gain_f * (mm(d_gate, user_gate, LAST) + mm(d_up, user_up, LAST))
    row_mean = jnp.mean(scaled * unit_rows, axis=1, keepdims=True)
    occ_part = (
        masked.astype(F32) * (1.0 / n_narrow) + inv_rms * (scaled - unit_rows * row_mean)
    ).astype(BF16)

    targets = item_row[hist_items.reshape(rows)]

    def item_rows_of(parity, first, count):
        blocks = jnp.arange(n_wide // 2, dtype=jnp.int32)[:, None] * 2 + parity
        ids = blocks * item_dev + first + jnp.arange(count, dtype=jnp.int32)[None, :]
        return ids.reshape(-1)

    def summed_rows(parity, first, count):
        one_hot = (item_rows_of(parity, first, count)[:, None] == targets[None, :]).astype(BF16)
        return mm(one_hot, occ_part)

    pieces = []
    for first, order in ((0, order_a), (half, order_b)):
        got = swap(summed_rows(1 - core, first, half).astype(BF16), "wide", 1)
        total = (summed_rows(core, first, half) + got.astype(F32)).astype(BF16)
        pieces.append(halve(total.reshape(cubes + (half, width)), order, me).astype(BF16))
    mine = jnp.concatenate(pieces, axis=0)
    quarter = item_dev // n_narrow

    def narrow_rows(value, which):
        return lax.dynamic_slice_in_dim(value, (which % n_narrow) * quarter, quarter, axis=0)

    def narrow_scatter(value):
        total = narrow_rows(value, here).astype(F32)
        for step in range(1, n_narrow):
            total = total + shift(narrow_rows(value, here + step), "narrow", step).astype(F32)
        return total

    def narrow_gather(piece):
        slots = [piece] + [shift(piece, "narrow", n_narrow - step) for step in range(1, n_narrow)]
        full = jnp.concatenate(slots + slots, axis=0)
        return lax.dynamic_slice_in_dim(full, ((n_narrow - here) % n_narrow) * quarter, item_dev, axis=0)

    item_in = narrow_scatter(mine)
    item_cot = narrow_gather(item_in.astype(BF16))

    all_cot = columns(item_cot)
    _, item_d_gate, item_d_up = grads(item_gate_act, item_up_act, mm(item_cot, item_down, LAST))
    all_d = gathered(jnp.concatenate([item_d_gate, item_d_up], axis=1))
    item_part = (mm(item_d_gate, item_gate, LAST) + mm(item_d_up, item_up, LAST)).astype(BF16)
    item_scaled = item_gain_f * narrow_scatter(item_part)
    own_unit, own_inv = narrow_rows(item_unit, here), narrow_rows(item_inv, here)
    item_mean = jnp.mean(item_scaled * own_unit, axis=1, keepdims=True)
    feat_grad = narrow_gather(
        (item_in + own_inv * (item_scaled - own_unit * item_mean)).astype(BF16)
    )
    item_both = mm(all_normed, all_d, FIRST) * (1.0 / n_wide)
    item_down_grad = mm(all_hidden, all_cot, FIRST) * (1.0 / n_wide)

    def by_core(value, parity):
        parts = value.reshape(rows, n_wide // 2, 2, block)
        return lax.dynamic_index_in_dim(parts, parity, axis=2, keepdims=False).reshape(rows, width // 2)

    def weight_grad(lhs_sent, lhs_kept, rhs):
        got = swap(mm(lhs_sent, rhs, FIRST).astype(BF16), "wide", 1)
        total = (mm(lhs_kept, rhs, FIRST) + got.astype(F32)).astype(BF16)
        total = total.reshape(cubes + (block, hid))
        cut = block // 2
        return jnp.concatenate(
            [
                halve(lax.slice_in_dim(total, 0, cut, axis=len(cubes)), order_a, me),
                halve(lax.slice_in_dim(total, cut, block, axis=len(cubes)), order_b, me),
            ],
            axis=0,
        ) * (1.0 / n_wide)

    normed_sent, normed_kept = by_core(normed, 1 - core), by_core(normed, core)
    masked_sent, masked_kept = by_core(masked, 1 - core), by_core(masked, core)
    user_gate_grad = weight_grad(normed_sent, normed_kept, d_gate)
    user_up_grad = weight_grad(normed_sent, normed_kept, d_up)
    user_down_grad = weight_grad(masked_sent, masked_kept, hidden).T
    return (
        feat_grad,
        user_gate_grad,
        user_up_grad,
        user_down_grad,
        item_both[:, :hid],
        item_both[:, hid:],
        item_down_grad,
    )


def solution(mesh):
    placed = (
        P("wide", None, None),
        P("wide", None, None),
        P("wide"),
        P("wide", None),
        P(),
        P("wide", None),
        P(),
        P(None, "narrow"),
        P(None, "narrow"),
        P("narrow", None),
        P(),
        P(None, "narrow"),
        P(None, "narrow"),
        P("narrow", None),
    )
    return jax.shard_map(
        body,
        mesh=mesh,
        in_specs=placed,
        out_specs=(
            P("wide", None),
            P("wide", "narrow"),
            P("wide", "narrow"),
            P("narrow", "wide"),
            P("wide", "narrow"),
            P("wide", "narrow"),
            P("narrow", "wide"),
        ),
        check_vma=False,
    )
```

```python
import functools

import jax
import jax.numpy as jnp
from jax import lax
from jax.experimental import pallas as pl
from jax.experimental.pallas import tpu as pltpu
from jax.sharding import PartitionSpec as P

F32 = jnp.float32
BF16 = jnp.bfloat16
LAST = (((1,), (1,)), ((), ()))
FIRST = (((0,), (0,)), ((), ()))
PLAIN = (((1,), (0,)), ((), ()))
TILE = 256
VMEM_BYTES = 58 * 1024 * 1024


def mm(a, b, dims=PLAIN):
    return lax.dot_general(a, b, dims, preferred_element_type=F32)


def params():
    return pltpu.CompilerParams(vmem_limit_bytes=VMEM_BYTES)


def cost(flops, touched):
    return pl.CostEstimate(flops=int(flops), bytes_accessed=int(touched), transcendentals=0)


def whole_spec(shape):
    return pl.BlockSpec(shape, lambda *_: (0,) * len(shape))


def swap(value, bit):
    count = lax.axis_size("wide")
    return lax.ppermute(value, "wide", [(i, i ^ bit) for i in range(count)])


def user_kernel(
    steps, share, x_ref, og_ref, valid_ref, gain_ref, gate_ref, up_ref, down_ref, target_ref,
    sent_ids_ref, kept_ids_ref,
    normed_out, masked_out, hidden_ref, d_gate_ref, d_up_ref, sent_ref, kept_ref,
    normed, masked, inv_ref, total, sems,
):
    step = pl.program_id(0)

    @pl.when(step == 0)
    def _():
        rows = x_ref[...].astype(F32)
        inv = lax.rsqrt(jnp.mean(rows * rows, axis=1, keepdims=True) + 1e-05)
        inv_ref[...] = inv
        normed[...] = (rows * inv * gain_ref[...].astype(F32)).astype(BF16)
        masked[...] = (og_ref[...].astype(F32) * valid_ref[...]).astype(BF16)
        pltpu.make_async_copy(normed, normed_out, sems.at[0]).start()
        pltpu.make_async_copy(masked, masked_out, sems.at[1]).start()

    gate_act = mm(normed[...], gate_ref[...])
    up_act = mm(normed[...], up_ref[...])
    d_hidden = mm(masked[...], down_ref[...], LAST)
    sig = 1.0 / (1.0 + jnp.exp(-gate_act))
    silu = gate_act * sig
    hidden_ref[...] = (silu * up_act).astype(BF16)
    d_up = (d_hidden * silu).astype(BF16)
    d_gate = (d_hidden * up_act * sig * (1.0 + gate_act * (1.0 - sig))).astype(BF16)
    d_up_ref[...] = d_up
    d_gate_ref[...] = d_gate
    part = mm(d_gate, gate_ref[...], LAST) + mm(d_up, up_ref[...], LAST)

    @pl.when(step == 0)
    def _():
        total[...] = part

    @pl.when(step > 0)
    def _():
        total[...] += part

    @pl.when(step == steps - 1)
    def _():
        inv = inv_ref[...]
        scaled = total[...] * gain_ref[...].astype(F32)
        unit = x_ref[...].astype(F32) * inv
        mean = jnp.mean(scaled * unit, axis=1, keepdims=True)
        occ = (masked[...].astype(F32) * share + inv * (scaled - unit * mean)).astype(BF16)
        targets = target_ref[...]
        sent_ref[...] = mm((sent_ids_ref[...] == targets).astype(BF16), occ).astype(BF16)
        kept_ref[...] = mm((kept_ids_ref[...] == targets).astype(BF16), occ).astype(BF16)
        pltpu.make_async_copy(normed, normed_out, sems.at[0]).wait()
        pltpu.make_async_copy(masked, masked_out, sems.at[1]).wait()


def user_layer(x, og, valid, gain, w_gate, w_up, w_down, targets, sent_ids, kept_ids, share):
    rows, width = x.shape
    hid = w_gate.shape[1]
    tile = min(TILE, hid)
    steps = hid // tile
    half = sent_ids.shape[0]
    columns = pl.BlockSpec((rows, tile), lambda s: (0, s))
    weights = pl.BlockSpec((width, tile), lambda s: (0, s))
    wide = jax.ShapeDtypeStruct((rows, width), BF16)
    narrow = jax.ShapeDtypeStruct((rows, hid), BF16)
    summed = jax.ShapeDtypeStruct((half, width), BF16)
    return pl.pallas_call(
        functools.partial(user_kernel, steps, share),
        grid=(steps,),
        in_specs=[
            whole_spec((rows, width)),
            whole_spec((rows, width)),
            whole_spec((rows, 1)),
            whole_spec((1, width)),
            weights,
            weights,
            pl.BlockSpec((tile, width), lambda s: (s, 0)),
            whole_spec((1, rows)),
            whole_spec((half, 1)),
            whole_spec((half, 1)),
        ],
        out_specs=[pl.BlockSpec(memory_space=pl.ANY)] * 2
        + [columns] * 3
        + [whole_spec((half, width))] * 2,
        out_shape=[wide, wide, narrow, narrow, narrow, summed, summed],
        scratch_shapes=[
            pltpu.VMEM((rows, width), BF16),
            pltpu.VMEM((rows, width), BF16),
            pltpu.VMEM((rows, 1), F32),
            pltpu.VMEM((rows, width), F32),
            pltpu.SemaphoreType.DMA((2,)),
        ],
        compiler_params=params(),
        cost_estimate=cost(10 * rows * width * hid, 20e6),
        name="user_layer",
    )(x, og, valid, gain, w_gate, w_up, w_down, targets, sent_ids, kept_ids)


def grad_rows(normed_ref, masked_ref, d_gate_ref, d_up_ref, hidden_ref):
    left, right = normed_ref[...], masked_ref[...]
    return (
        mm(left, d_gate_ref[...], FIRST),
        mm(left, d_up_ref[...], FIRST),
        mm(right, hidden_ref[...], FIRST),
    )


def sent_kernel(table_ref, normed_ref, masked_ref, d_gate_ref, d_up_ref, hidden_ref, out_ref):
    hid = hidden_ref.shape[1]
    found = grad_rows(normed_ref, masked_ref, d_gate_ref, d_up_ref, hidden_ref)
    for k, piece in enumerate(found):
        out_ref[0, :, k * hid : (k + 1) * hid] = piece.astype(BF16)


def kept_kernel(
    table_ref, normed_ref, masked_ref, d_gate_ref, d_up_ref, hidden_ref, got_ref,
    sent_a, kept_a, sent_b, kept_b,
):
    step = pl.program_id(0)
    hid = hidden_ref.shape[1]
    cut = got_ref.shape[1] // 2
    found = grad_rows(normed_ref, masked_ref, d_gate_ref, d_up_ref, hidden_ref)
    for first, sent, kept, flag in ((0, sent_a, kept_a, 3), (cut, sent_b, kept_b, 6)):
        for k, piece in enumerate(found):
            at = slice(k * hid, (k + 1) * hid)
            value = piece[first : first + cut] + got_ref[0, first : first + cut, at].astype(F32)
            value = value.astype(BF16)

            @pl.when(table_ref[flag, step] == 1)
            def _(sent=sent, value=value, at=at):
                sent[0, :, at] = value

            @pl.when(table_ref[flag, step] == 0)
            def _(kept=kept, value=value, at=at):
                kept[0, :, at] = value


def lhs_specs(rows, block, hid):
    if block % 128:
        column = pl.BlockSpec((None, rows, block), lambda s, t: (s, 0, 0))
    else:
        column = pl.BlockSpec((rows, block), lambda s, t: (0, t[0, s]))
    return [column, column] + [whole_spec((rows, hid))] * 3


def lhs_arrays(table, normed, masked, block):
    if block % 128 == 0:
        return normed, masked
    return tuple(
        jnp.take(jnp.swapaxes(a.reshape(a.shape[0], -1, block), 0, 1), table[0], axis=0)
        for a in (normed, masked)
    )


def sent_grads(table, normed, masked, d_gate, d_up, hidden, block):
    rows, hid = hidden.shape
    count = table.shape[1]
    return pl.pallas_call(
        sent_kernel,
        grid_spec=pltpu.PrefetchScalarGridSpec(
            num_scalar_prefetch=1,
            grid=(count,),
            in_specs=lhs_specs(rows, block, hid),
            out_specs=pl.BlockSpec((1, block, 3 * hid), lambda s, t: (s, 0, 0)),
        ),
        out_shape=jax.ShapeDtypeStruct((count, block, 3 * hid), BF16),
        compiler_params=params(),
        cost_estimate=cost(6 * rows * block * count * hid, 10e6),
        name="sent_grads",
    )(table, *lhs_arrays(table, normed, masked, block), d_gate, d_up, hidden)


def kept_grads(table, normed, masked, d_gate, d_up, hidden, got, block):
    rows, hid = hidden.shape
    count = table.shape[1]
    piece = jax.ShapeDtypeStruct((count // 2, block // 2, 3 * hid), BF16)

    def out(row):
        return pl.BlockSpec((1, block // 2, 3 * hid), lambda s, t: (t[row, s], 0, 0))

    return pl.pallas_call(
        kept_kernel,
        grid_spec=pltpu.PrefetchScalarGridSpec(
            num_scalar_prefetch=1,
            grid=(count,),
            in_specs=lhs_specs(rows, block, hid)
            + [pl.BlockSpec((1, block, 3 * hid), lambda s, t: (t[7, s], 0, 0))],
            out_specs=[out(1), out(2), out(4), out(5)],
        ),
        out_shape=[piece] * 4,
        compiler_params=params(),
        cost_estimate=cost(6 * rows * block * count * hid, 15e6),
        name="kept_grads",
    )(table, *lhs_arrays(table, normed, masked, block), d_gate, d_up, hidden, got)


def forward_kernel(x_ref, gain_ref, gate_ref, up_ref, slope_up, slope_gate, hidden_ref, normed_out, normed):
    @pl.when(pl.program_id(0) == 0)
    def _():
        rows = x_ref[...].astype(F32)
        inv = lax.rsqrt(jnp.mean(rows * rows, axis=1, keepdims=True) + 1e-05)
        normed[...] = (rows * inv * gain_ref[...].astype(F32)).astype(BF16)
        normed_out[...] = normed[...]

    gate_act = mm(normed[...], gate_ref[...])
    up_act = mm(normed[...], up_ref[...])
    sig = 1.0 / (1.0 + jnp.exp(-gate_act))
    silu = gate_act * sig
    hidden_ref[...] = (silu * up_act).astype(BF16)
    slope_up[...] = silu.astype(BF16)
    slope_gate[...] = (up_act * sig * (1.0 + gate_act * (1.0 - sig))).astype(BF16)


def item_forward(x, gain, w_gate, w_up):
    rows, width = x.shape
    hid = w_gate.shape[1]
    tile = min(TILE, hid)
    weights = pl.BlockSpec((width, tile), lambda s: (0, s))
    columns = pl.BlockSpec((rows, tile), lambda s: (0, s))
    narrow = jax.ShapeDtypeStruct((rows, hid), BF16)
    return pl.pallas_call(
        forward_kernel,
        grid=(hid // tile,),
        in_specs=[whole_spec((rows, width)), whole_spec((1, width)), weights, weights],
        out_specs=[columns] * 3 + [whole_spec((rows, width))],
        out_shape=[narrow] * 3 + [jax.ShapeDtypeStruct((rows, width), BF16)],
        scratch_shapes=[pltpu.VMEM((rows, width), BF16)],
        compiler_params=params(),
        cost_estimate=cost(4 * rows * width * hid, 12e6),
        name="item_forward",
    )(x, gain, w_gate, w_up)


def own_kernel(cot_ref, slope_up, slope_gate, gate_ref, up_ref, down_ref, out_ref, total):
    step = pl.program_id(0)
    d_hidden = mm(cot_ref[...], down_ref[...], LAST)
    d_up = (d_hidden * slope_up[...].astype(F32)).astype(BF16)
    d_gate = (d_hidden * slope_gate[...].astype(F32)).astype(BF16)
    part = mm(d_gate, gate_ref[...], LAST) + mm(d_up, up_ref[...], LAST)

    @pl.when(step == 0)
    def _():
        total[...] = part

    @pl.when(step > 0)
    def _():
        total[...] += part

    @pl.when(step == pl.num_programs(0) - 1)
    def _():
        out_ref[...] = total[...].astype(BF16)


def item_own(cot, slope_up, slope_gate, w_gate, w_up, w_down):
    rows, width = cot.shape
    hid = w_gate.shape[1]
    tile = min(TILE, hid)
    weights = pl.BlockSpec((width, tile), lambda s: (0, s))
    columns = pl.BlockSpec((rows, tile), lambda s: (0, s))
    return pl.pallas_call(
        own_kernel,
        grid=(hid // tile,),
        in_specs=[
            whole_spec((rows, width)),
            columns,
            columns,
            weights,
            weights,
            pl.BlockSpec((tile, width), lambda s: (s, 0)),
        ],
        out_specs=whole_spec((rows, width)),
        out_shape=jax.ShapeDtypeStruct((rows, width), BF16),
        scratch_shapes=[pltpu.VMEM((rows, width), F32)],
        compiler_params=params(),
        cost_estimate=cost(6 * rows * width * hid, 11e6),
        name="item_own",
    )(cot, slope_up, slope_gate, w_gate, w_up, w_down)


def late_kernel(
    scale, at_ref, cot0, cot1, col0, col1, n0, n1, su0, su1, sg0, sg1, h0, h1, down_ref,
    gate_out, up_out, down_out,
):
    sums = None
    for cot, col, normed, su, sg, hidden in ((cot0, col0, n0, su0, sg0, h0), (cot1, col1, n1, su1, sg1, h1)):
        d_hidden = mm(cot[...], down_ref[...], LAST)
        d_up = (d_hidden * su[...].astype(F32)).astype(BF16)
        d_gate = (d_hidden * sg[...].astype(F32)).astype(BF16)
        found = (
            mm(normed[...], d_gate, FIRST),
            mm(normed[...], d_up, FIRST),
            mm(hidden[...], col[...], FIRST),
        )
        sums = found if sums is None else tuple(a + b for a, b in zip(sums, found))
    gate_out[...] = sums[0] * scale
    up_out[...] = sums[1] * scale
    down_out[...] = sums[2] * scale


def item_late(me, cots, normeds, slope_ups, slope_gates, hiddens, w_down, block, scale):
    rows, width = cots[0].shape
    hid = w_down.shape[0]
    tile = min(TILE, hid)
    full = pl.BlockSpec((rows, width), lambda s, t: (0, 0))
    columns_of = list(cots) + list(normeds)
    if block % 128:
        mine = pl.BlockSpec((rows, block), lambda s, t: (0, 0))
        columns_of = [lax.dynamic_slice_in_dim(a, me * block, block, axis=1) for a in columns_of]
    else:
        mine = pl.BlockSpec((rows, block), lambda s, t: (0, t[0]))
    columns = pl.BlockSpec((rows, tile), lambda s, t: (0, s))
    out = pl.BlockSpec((block, tile), lambda s, t: (0, s))
    return pl.pallas_call(
        functools.partial(late_kernel, scale),
        grid_spec=pltpu.PrefetchScalarGridSpec(
            num_scalar_prefetch=1,
            grid=(hid // tile,),
            in_specs=[full, full, mine, mine, mine, mine]
            + [columns] * 6
            + [pl.BlockSpec((tile, width), lambda s, t: (s, 0))],
            out_specs=[out, out, pl.BlockSpec((tile, block), lambda s, t: (s, 0))],
        ),
        out_shape=[
            jax.ShapeDtypeStruct((block, hid), F32),
            jax.ShapeDtypeStruct((block, hid), F32),
            jax.ShapeDtypeStruct((hid, block), F32),
        ],
        compiler_params=params(),
        cost_estimate=cost(4 * rows * width * hid + 12 * rows * block * hid, 16e6),
        name="item_late",
    )(jnp.reshape(me, (1,)), *cots, *columns_of, *slope_ups, *slope_gates, *hiddens, w_down)


def grad_tables(n_chips, chip, core, order_a, order_b):
    first_a, first_b = order_a[0] >> 1, order_b[0] >> 1
    rels = sorted(range(n_chips), key=lambda r: (not (r & first_a), not (r & first_b), r))
    rows = [[], [], [], [], [], [], []]
    places = {}
    for name, first, row in (("a", first_a, 0), ("b", first_b, 3)):
        sent_order = [r for r in rels if r & first]
        kept_order = [r for r in rels if not r & first]
        last_sent = last_kept = 0
        for r in rels:
            is_sent = bool(r & first)
            if is_sent:
                last_sent = sent_order.index(r)
            else:
                last_kept = kept_order.index(r)
            rows[row].append(last_sent)
            rows[row + 1].append(last_kept)
            rows[row + 2].append(int(is_sent))
        places[name] = kept_order
    rel = jnp.array(rels, jnp.int32)
    fixed = [jnp.array(r, jnp.int32) for r in rows[:6]]
    table = jnp.stack([(chip ^ rel) * 2 + core, *fixed, rel])
    return table, places


def finish_halving(sent, kept, order, slots):
    got = swap(sent, order[0])
    total = {r: kept[i].astype(F32) + got[i].astype(F32) for i, r in enumerate(slots)}
    for bit in order[1:]:
        away = sorted(r for r in total if r & (bit >> 1))
        block = jnp.stack([total[r].astype(BF16) for r in away])
        got = swap(block, bit)
        total = {
            r ^ (bit >> 1): total[r ^ (bit >> 1)].astype(BF16).astype(F32) + got[i].astype(F32)
            for i, r in enumerate(away)
        }
    return total[0]


def body(
    user_input,
    out_grad,
    hist_len,
    hist_items,
    item_row,
    item_feat,
    user_gain,
    user_gate,
    user_up,
    user_down,
    item_gain,
    item_gate,
    item_up,
    item_down,
):
    n_wide, n_narrow = lax.axis_size("wide"), lax.axis_size("narrow")
    me, here = lax.axis_index("wide"), lax.axis_index("narrow")
    chip, core = me // 2, me % 2
    n_chips = n_wide // 2
    bits = [1 << k for k in range(1, n_wide.bit_length() - 1)]
    order_a = bits
    order_b = bits[len(bits) // 2 :] + bits[: len(bits) // 2]
    user_count, hist_length, width = user_input.shape
    rows = user_count * hist_length
    item_dev = item_feat.shape[0]
    hid = user_gate.shape[1]
    block = width // n_wide
    rels = jnp.arange(n_chips, dtype=jnp.int32)
    gain_user, gain_item = user_gain.reshape(1, width), item_gain.reshape(1, width)

    def gather_wide(value):
        near = jnp.concatenate([value] + [swap(value, r << 1) for r in range(1, n_chips)], axis=0)
        return near, swap(near, 1)

    feats = gather_wide(item_feat)

    valid = (jnp.arange(hist_length, dtype=jnp.int32)[None, :] < hist_len[:, None]).astype(F32)
    ids = jnp.arange(item_row.shape[0], dtype=jnp.int32)
    targets = jnp.sum(
        jnp.where(hist_items.reshape(rows)[:, None] == ids[None, :], item_row[None, :], 0), axis=1
    )

    def item_ids(parity):
        first = ((chip ^ rels) * 2 + parity) * item_dev
        return (first[:, None] + jnp.arange(item_dev, dtype=jnp.int32)[None, :]).reshape(-1, 1)

    normed, masked, hidden, d_gate, d_up, sent, kept = user_layer(
        user_input.reshape(rows, width),
        out_grad.reshape(rows, width),
        valid.reshape(rows, 1),
        gain_user,
        user_gate,
        user_up,
        user_down,
        targets.reshape(1, rows),
        item_ids(1 - core),
        item_ids(core),
        1.0 / n_narrow,
    )

    got = swap(sent, 1)
    pieces = []
    for r in range(n_chips):
        at = slice(r * item_dev, (r + 1) * item_dev)
        piece = kept[at].astype(F32) + got[at].astype(F32)
        pieces.append(piece if r == 0 else swap(piece.astype(BF16), r << 1))
    mine = functools.reduce(jnp.add, [p.astype(F32) for p in pieces]).astype(BF16)

    sent_table = jnp.stack([(chip ^ rels) * 2 + 1 - core])
    kept_table, places = grad_tables(n_chips, chip, core, order_a, order_b)
    grads_got = swap(sent_grads(sent_table, normed, masked, d_gate, d_up, hidden, block), 1)
    sent_a, kept_a, sent_b, kept_b = kept_grads(
        kept_table, normed, masked, d_gate, d_up, hidden, grads_got, block
    )
    user_grads = jnp.concatenate(
        [
            finish_halving(sent_a, kept_a, order_a, places["a"]),
            finish_halving(sent_b, kept_b, order_b, places["b"]),
        ],
        axis=0,
    ) * (1.0 / n_wide)

    quarter = item_dev // n_narrow

    def narrow_rows(value):
        return lax.dynamic_slice_in_dim(value, here * quarter, quarter, axis=0)

    def narrow_scatter(value):
        parts = lax.all_to_all(
            value.reshape(n_narrow, quarter, width), "narrow", split_axis=0, concat_axis=0, tiled=True
        )
        return jnp.sum(parts.astype(F32), axis=0)

    def narrow_gather(piece):
        return lax.all_gather(piece, "narrow", axis=0, tiled=True)

    forwards = [item_forward(x, gain_item, item_gate, item_up) for x in feats]
    slope_ups, slope_gates, hiddens, normeds = zip(*forwards)

    item_in = narrow_scatter(mine)
    item_cot = narrow_gather(item_in.astype(BF16))
    cots = gather_wide(item_cot)
    item_part = item_own(
        item_cot, slope_ups[0][:item_dev], slope_gates[0][:item_dev], item_gate, item_up, item_down
    )
    item_scaled = gain_item.astype(F32) * narrow_scatter(item_part)
    own = narrow_rows(item_feat).astype(F32)
    own_inv = lax.rsqrt(jnp.mean(own * own, axis=1, keepdims=True) + 1e-05)
    own_unit = own * own_inv
    item_mean = jnp.mean(item_scaled * own_unit, axis=1, keepdims=True)
    feat_grad = narrow_gather(
        (item_in + own_inv * (item_scaled - own_unit * item_mean)).astype(BF16)
    )
    item_gate_grad, item_up_grad, item_down_grad = item_late(
        me, cots, normeds, slope_ups, slope_gates, hiddens, item_down, block, 1.0 / n_wide
    )
    return (
        feat_grad,
        user_grads[:, :hid],
        user_grads[:, hid : 2 * hid],
        user_grads[:, 2 * hid :].T,
        item_gate_grad,
        item_up_grad,
        item_down_grad,
    )


def solution(mesh):
    placed = (
        P("wide", None, None),
        P("wide", None, None),
        P("wide"),
        P("wide", None),
        P(),
        P("wide", None),
        P(),
        P(None, "narrow"),
        P(None, "narrow"),
        P("narrow", None),
        P(),
        P(None, "narrow"),
        P(None, "narrow"),
        P("narrow", None),
    )
    return jax.shard_map(
        body,
        mesh=mesh,
        in_specs=placed,
        out_specs=(
            P("wide", None),
            P("wide", "narrow"),
            P("wide", "narrow"),
            P("narrow", "wide"),
            P("wide", "narrow"),
            P("wide", "narrow"),
            P("narrow", "wide"),
        ),
        check_vma=False,
    )
```

```python
import functools

import jax
import jax.numpy as jnp
from jax import lax
from jax.experimental import pallas as pl
from jax.experimental.pallas import tpu as pltpu
from jax.sharding import PartitionSpec as P

F32 = jnp.float32
BF16 = jnp.bfloat16
LAST = (((1,), (1,)), ((), ()))
FIRST = (((0,), (0,)), ((), ()))
PLAIN = (((1,), (0,)), ((), ()))
TILE = 256


def mm(a, b, dims=PLAIN):
    return lax.dot_general(a, b, dims, preferred_element_type=F32)


def params():
    return pltpu.CompilerParams(vmem_limit_bytes=60 << 20)


def cost(flops, touched):
    return pl.CostEstimate(flops=int(flops) // 6, bytes_accessed=int(touched) // 6, transcendentals=0)


def hbm():
    return pl.BlockSpec(memory_space=pl.ANY)


def vmem():
    return pl.BlockSpec(memory_space=pltpu.VMEM)


def smem():
    return pl.BlockSpec(memory_space=pltpu.SMEM)


def whole_spec(shape):
    return pl.BlockSpec(shape, lambda *_: (0,) * len(shape))


def swap(value, bit):
    count = lax.axis_size("wide")
    return lax.ppermute(value, "wide", [(i, i ^ bit) for i in range(count)])


def after(value, *others):
    return lax.optimization_barrier((value, *others))[0]


def tiles(total, size):
    size = min(size, total)
    return [slice(k, k + size) for k in range(0, total, size)]


def segment_picks(place, parity, targets, item_dev, count):
    column = lax.broadcasted_iota(jnp.int32, (1, count), 1)
    block = (place ^ (column // item_dev)) * 2 + parity
    return (targets == block * item_dev + column % item_dev).astype(BF16)


def user_kernel(
    share, item_dev, place_ref, hist_len_ref, x_hbm, og_hbm, hist_ref, item_row_ref, gain_ref,
    gate_hbm, up_hbm, down_hbm,
    normed_out, masked_out, hidden_out, d_gate_out, d_up_out, sent_out, kept_out,
    x, og, gate, up, down, normed, hidden, d_gate, d_up, gate_act, up_act, total, sent, kept, inv_ref,
    sems,
):
    loads = [
        pltpu.make_async_copy(src, dst, sems.at[k])
        for k, (src, dst) in enumerate(
            ((x_hbm, x), (gate_hbm, gate), (up_hbm, up), (og_hbm, og), (down_hbm, down))
        )
    ]
    for load in loads[:2]:
        load.start()
    stores = [
        pltpu.make_async_copy(src, dst, sems.at[5 + k])
        for k, (src, dst) in enumerate(
            (
                (normed, normed_out),
                (og, masked_out),
                (hidden, hidden_out),
                (d_gate, d_gate_out),
                (d_up, d_up_out),
            )
        )
    ]
    rows, width = x.shape
    users, length = hist_ref.shape
    hid = hidden.shape[1]
    gain = gain_ref[...].reshape(1, width).astype(F32)

    square = (length, length)
    diagonal = lax.broadcasted_iota(jnp.int32, square, 0) == lax.broadcasted_iota(jnp.int32, square, 1)
    item_row = item_row_ref[...].reshape(1, -1)
    ids = lax.broadcasted_iota(jnp.int32, (1, item_row.shape[1]), 1)
    targets = []
    for u in range(users):
        items = jnp.sum(jnp.where(diagonal, hist_ref[u : u + 1, :], 0), axis=1, keepdims=True)
        targets.append(jnp.sum(jnp.where(items == ids, item_row, 0), axis=1, keepdims=True))
    targets = jnp.concatenate(targets, axis=0)

    loads[0].wait()
    for load in loads[2:]:
        load.start()
    for at in tiles(rows, 64):
        part = x[at, :].astype(F32)
        inv = lax.rsqrt(jnp.mean(part * part, axis=1, keepdims=True) + 1e-05)
        inv_ref[at, :] = inv
        normed[at, :] = (part * inv * gain).astype(BF16)
    stores[0].start()
    loads[1].wait()
    for at in tiles(hid, TILE):
        gate_act[:, at] = mm(normed[...], gate[:, at])
    loads[2].wait()
    for at in tiles(hid, TILE):
        up_act[:, at] = mm(normed[...], up[:, at])
    loads[3].wait()
    place = lax.broadcasted_iota(jnp.int32, (length, 1), 0)
    for u in range(users):
        at = slice(u * length, (u + 1) * length)
        og[at, :] = jnp.where(place < hist_len_ref[u], og[at, :].astype(F32), 0.0).astype(BF16)
    stores[1].start()
    loads[4].wait()
    for at in tiles(hid, TILE):
        d_hidden = mm(og[...], down[at, :], LAST)
        gate_part, up_part = gate_act[:, at], up_act[:, at]
        sig = 1.0 / (1.0 + jnp.exp(-gate_part))
        silu = gate_part * sig
        hidden[:, at] = (silu * up_part).astype(BF16)
        d_up[:, at] = (d_hidden * silu).astype(BF16)
        d_gate[:, at] = (d_hidden * up_part * sig * (1.0 + gate_part * (1.0 - sig))).astype(BF16)
    for k in (2, 3, 4):
        stores[k].start()
    mean = jnp.zeros((rows, 1), F32)
    inv = inv_ref[...]
    for at in tiles(width, 512):
        part = mm(d_gate[...], gate[at, :], LAST) + mm(d_up[...], up[at, :], LAST)
        part = part * gain[:, at]
        total[:, at] = part
        mean = mean + jnp.sum(part * (x[:, at].astype(F32) * inv), axis=1, keepdims=True)
    slope = inv * inv * mean * (1.0 / width)
    chip, core = place_ref[0], place_ref[1]
    half = sent.shape[0]
    picks_sent = segment_picks(chip, 1 - core, targets, item_dev, half)
    picks_kept = segment_picks(chip, core, targets, item_dev, half)
    for at in tiles(width, 512):
        occ = (
            og[:, at].astype(F32) * share + inv * total[:, at] - x[:, at].astype(F32) * slope
        ).astype(BF16)
        sent[:, at] = mm(picks_sent, occ, FIRST).astype(BF16)
        kept[:, at] = mm(picks_kept, occ, FIRST).astype(BF16)
        for src, dst in ((sent, sent_out), (kept, kept_out)):
            stores.append(pltpu.make_async_copy(src.at[:, at], dst.at[:, at], sems.at[5 + len(stores)]))
            stores[-1].start()
    for store in stores:
        store.wait()


def user_layer(place, hist_len, x, og, hist, item_row, gain, w_gate, w_up, w_down, share, item_dev):
    rows, width = x.shape
    hid = w_gate.shape[1]
    half = item_row.shape[0] // 2
    wide = jax.ShapeDtypeStruct((rows, width), BF16)
    narrow = jax.ShapeDtypeStruct((rows, hid), BF16)
    summed = jax.ShapeDtypeStruct((half, width), BF16)
    return pl.pallas_call(
        functools.partial(user_kernel, share, item_dev),
        in_specs=[smem()] * 2 + [hbm()] * 2 + [vmem()] * 3 + [hbm()] * 3,
        out_specs=[hbm()] * 7,
        out_shape=[wide, wide, narrow, narrow, narrow, summed, summed],
        scratch_shapes=[
            pltpu.VMEM((rows, width), BF16),
            pltpu.VMEM((rows, width), BF16),
            pltpu.VMEM((width, hid), BF16),
            pltpu.VMEM((width, hid), BF16),
            pltpu.VMEM((hid, width), BF16),
            pltpu.VMEM((rows, width), BF16),
            pltpu.VMEM((rows, hid), BF16),
            pltpu.VMEM((rows, hid), BF16),
            pltpu.VMEM((rows, hid), BF16),
            pltpu.VMEM((rows, hid), F32),
            pltpu.VMEM((rows, hid), F32),
            pltpu.VMEM((rows, width), F32),
            pltpu.VMEM((half, width), BF16),
            pltpu.VMEM((half, width), BF16),
            pltpu.VMEM((rows, 1), F32),
            pltpu.SemaphoreType.DMA((10 + 2 * len(tiles(width, 512)),)),
        ],
        compiler_params=params(),
        cost_estimate=cost(10 * rows * width * hid, 24e6),
        name="user_layer",
    )(place, hist_len, x, og, hist, item_row, gain, w_gate, w_up, w_down)


def grad_rows(normed_ref, masked_ref, d_gate_ref, d_up_ref, hidden_ref):
    left, right = normed_ref[...], masked_ref[...]
    return (
        mm(left, d_gate_ref[...], FIRST),
        mm(left, d_up_ref[...], FIRST),
        mm(right, hidden_ref[...], FIRST),
    )


def sent_kernel(table_ref, normed_ref, masked_ref, d_gate_ref, d_up_ref, hidden_ref, out_ref):
    hid = hidden_ref.shape[1]
    found = grad_rows(normed_ref, masked_ref, d_gate_ref, d_up_ref, hidden_ref)
    for k, piece in enumerate(found):
        out_ref[0, :, k * hid : (k + 1) * hid] = piece.astype(BF16)


def kept_kernel(
    table_ref, normed_ref, masked_ref, d_gate_ref, d_up_ref, hidden_ref, got_ref,
    sent_a, kept_a, sent_b, kept_b,
):
    step = pl.program_id(0)
    hid = hidden_ref.shape[1]
    cut = got_ref.shape[1] // 2
    found = grad_rows(normed_ref, masked_ref, d_gate_ref, d_up_ref, hidden_ref)
    for first, sent, kept, flag in ((0, sent_a, kept_a, 3), (cut, sent_b, kept_b, 6)):
        for k, piece in enumerate(found):
            at = slice(k * hid, (k + 1) * hid)
            value = piece[first : first + cut] + got_ref[0, first : first + cut, at].astype(F32)
            value = value.astype(BF16)

            @pl.when(table_ref[flag, step] == 1)
            def _(sent=sent, value=value, at=at):
                sent[0, :, at] = value

            @pl.when(table_ref[flag, step] == 0)
            def _(kept=kept, value=value, at=at):
                kept[0, :, at] = value


def lhs_specs(rows, block, hid):
    if block % 128:
        column = pl.BlockSpec((None, rows, block), lambda s, t: (s, 0, 0))
    else:
        column = pl.BlockSpec((rows, block), lambda s, t: (0, t[0, s]))
    return [column, column] + [whole_spec((rows, hid))] * 3


def lhs_arrays(table, normed, masked, block):
    if block % 128 == 0:
        return normed, masked
    return tuple(
        jnp.take(jnp.swapaxes(a.reshape(a.shape[0], -1, block), 0, 1), table[0], axis=0)
        for a in (normed, masked)
    )


def sent_grads(table, normed, masked, d_gate, d_up, hidden, block):
    rows, hid = hidden.shape
    count = table.shape[1]
    return pl.pallas_call(
        sent_kernel,
        grid_spec=pltpu.PrefetchScalarGridSpec(
            num_scalar_prefetch=1,
            grid=(count,),
            in_specs=lhs_specs(rows, block, hid),
            out_specs=pl.BlockSpec((1, block, 3 * hid), lambda s, t: (s, 0, 0)),
        ),
        out_shape=jax.ShapeDtypeStruct((count, block, 3 * hid), BF16),
        compiler_params=params(),
        cost_estimate=cost(6 * rows * block * count * hid, 10e6),
        name="sent_grads",
    )(table, *lhs_arrays(table, normed, masked, block), d_gate, d_up, hidden)


def kept_grads(table, normed, masked, d_gate, d_up, hidden, got, block):
    rows, hid = hidden.shape
    count = table.shape[1]
    piece = jax.ShapeDtypeStruct((count // 2, block // 2, 3 * hid), BF16)

    def out(row):
        return pl.BlockSpec((1, block // 2, 3 * hid), lambda s, t: (t[row, s], 0, 0))

    return pl.pallas_call(
        kept_kernel,
        grid_spec=pltpu.PrefetchScalarGridSpec(
            num_scalar_prefetch=1,
            grid=(count,),
            in_specs=lhs_specs(rows, block, hid)
            + [pl.BlockSpec((1, block, 3 * hid), lambda s, t: (t[7, s], 0, 0))],
            out_specs=[out(1), out(2), out(4), out(5)],
        ),
        out_shape=[piece] * 4,
        compiler_params=params(),
        cost_estimate=cost(6 * rows * block * count * hid, 15e6),
        name="kept_grads",
    )(table, *lhs_arrays(table, normed, masked, block), d_gate, d_up, hidden, got)


def forward_kernel(count, place_ref, gain_ref, *refs):
    feats, (gate_hbm, up_hbm) = refs[:count], refs[count : count + 2]
    normed_out, hidden_out, slope_up_out, slope_gate_out = refs[count + 2 : count + 6]
    x, normed, gate, up, gate_act, hidden, slope_up, slope_gate, sems = refs[count + 6 :]
    width, hid = gate.shape
    all_rows = x.shape[0]
    rows = all_rows // count
    pieces = [
        pltpu.make_async_copy(feats[k], x.at[pl.ds(k * rows, rows)], sems.at[k]) for k in range(count)
    ]
    gate_load = pltpu.make_async_copy(gate_hbm, gate, sems.at[count])
    up_load = pltpu.make_async_copy(up_hbm, up, sems.at[count + 1])
    halves = [range(count // 2), range(count // 2, count)]
    for k in halves[0]:
        pieces[k].start()
    gate_load.start()
    gain = gain_ref[...].reshape(1, width).astype(F32)

    def normalise(k):
        for at in tiles(rows, 64):
            at = slice(k * rows + at.start, k * rows + at.stop)
            part = x[at, :].astype(F32)
            inv = lax.rsqrt(jnp.mean(part * part, axis=1, keepdims=True) + 1e-05)
            normed[at, :] = (part * inv * gain).astype(BF16)

    for k in halves[0]:
        pieces[k].wait()
    for k in halves[1]:
        pieces[k].start()
    up_load.start()
    for k in halves[0]:
        normalise(k)
    gate_load.wait()
    for h in range(2):
        part = slice(h * all_rows // 2, (h + 1) * all_rows // 2)
        if h == 1:
            for k in halves[1]:
                pieces[k].wait()
            for k in halves[1]:
                normalise(k)
        for at in tiles(hid, TILE):
            gate_act[part, at] = mm(normed[part, :], gate[:, at])
    block = normed_out.shape[1]
    mine = normed
    if block < width:
        mine = normed.at[:, pl.ds(pl.multiple_of(place_ref[2] * block, 128), block)]
    stores = [pltpu.make_async_copy(mine, normed_out, sems.at[count + 2])]
    stores[0].start()
    up_load.wait()
    for at in tiles(hid, TILE):
        up_part = mm(normed[...], up[:, at])
        gate_part = gate_act[:, at]
        sig = 1.0 / (1.0 + jnp.exp(-gate_part))
        silu = gate_part * sig
        hidden[:, at] = (silu * up_part).astype(BF16)
        slope_up[:, at] = silu.astype(BF16)
        slope_gate[:, at] = (up_part * sig * (1.0 + gate_part * (1.0 - sig))).astype(BF16)
        for src, dst in ((hidden, hidden_out), (slope_up, slope_up_out), (slope_gate, slope_gate_out)):
            sem = sems.at[count + 2 + len(stores)]
            stores.append(pltpu.make_async_copy(src.at[:, at], dst.at[:, at], sem))
            stores[-1].start()
    for store in stores:
        store.wait()


def item_forward(place, gain, feats, w_gate, w_up, block):
    count = len(feats)
    rows, width = count * feats[0].shape[0], feats[0].shape[1]
    hid = w_gate.shape[1]
    kept = width if block % 128 else block
    narrow = jax.ShapeDtypeStruct((rows, hid), BF16)
    return pl.pallas_call(
        functools.partial(forward_kernel, count),
        in_specs=[smem(), vmem()] + [hbm()] * (count + 2),
        out_specs=[hbm()] * 4,
        out_shape=[jax.ShapeDtypeStruct((rows, kept), BF16)] + [narrow] * 3,
        scratch_shapes=[
            pltpu.VMEM((rows, width), BF16),
            pltpu.VMEM((rows, width), BF16),
            pltpu.VMEM((width, hid), BF16),
            pltpu.VMEM((width, hid), BF16),
            pltpu.VMEM((rows, hid), F32),
            pltpu.VMEM((rows, hid), BF16),
            pltpu.VMEM((rows, hid), BF16),
            pltpu.VMEM((rows, hid), BF16),
            pltpu.SemaphoreType.DMA((count + 3 + 3 * len(tiles(hid, TILE)),)),
        ],
        compiler_params=params(),
        cost_estimate=cost(4 * rows * width * hid, 16e6),
        name="item_forward",
    )(place, gain, *feats, w_gate, w_up)


def own_kernel(
    cot, slope_up, slope_gate, gate_hbm, up_hbm, down_hbm, out_ref, gate, up, down, sems
):
    loads = [
        pltpu.make_async_copy(src, dst, sems.at[k])
        for k, (src, dst) in enumerate(((down_hbm, down), (gate_hbm, gate), (up_hbm, up)))
    ]
    for load in loads:
        load.start()
    loads[0].wait()
    d_hidden = mm(cot[...], down[...], LAST)
    d_up = (d_hidden * slope_up[...].astype(F32)).astype(BF16)
    d_gate = (d_hidden * slope_gate[...].astype(F32)).astype(BF16)
    loads[1].wait()
    loads[2].wait()
    for at in tiles(out_ref.shape[1], 512):
        out_ref[:, at] = (mm(d_gate, gate[at, :], LAST) + mm(d_up, up[at, :], LAST)).astype(BF16)


def item_own(cot, slope_up, slope_gate, w_gate, w_up, w_down):
    rows, width = cot.shape
    hid = w_gate.shape[1]
    return pl.pallas_call(
        own_kernel,
        grid=(1,),
        in_specs=[whole_spec((rows, width)), whole_spec((rows, hid)), whole_spec((rows, hid))]
        + [hbm()] * 3,
        out_specs=whole_spec((rows, width)),
        out_shape=jax.ShapeDtypeStruct((rows, width), BF16),
        scratch_shapes=[
            pltpu.VMEM((width, hid), BF16),
            pltpu.VMEM((width, hid), BF16),
            pltpu.VMEM((hid, width), BF16),
            pltpu.SemaphoreType.DMA((3,)),
        ],
        compiler_params=params(),
        cost_estimate=cost(6 * rows * width * hid, 11e6),
        name="item_own",
    )(cot, slope_up, slope_gate, w_gate, w_up, w_down)


def late_kernel(count, scale, place_ref, *refs):
    pieces, (column_hbm, normed_hbm, hidden_hbm, slope_up_hbm, slope_gate_hbm, down_hbm) = (
        refs[:count],
        refs[count : count + 6],
    )
    gate_out, up_out, down_out = refs[count + 6 : count + 9]
    cot, column, normed, hidden, slope_up, slope_gate, down, sems = refs[count + 9 :]
    rows = cot.shape[0] // count
    half = cot.shape[0] // 2
    used = 0

    def load(src, dst):
        nonlocal used
        copy = pltpu.make_async_copy(src, dst, sems.at[used])
        used += 1
        return copy

    narrow = normed.shape[1] % 128 != 0
    parts = []
    down_load = load(down_hbm, down)
    for h in range(2):
        at = pl.ds(h * half, half)
        waits = [
            load(pieces[k], cot.at[pl.ds(k * rows, rows)])
            for k in range(h * count // 2, (h + 1) * count // 2)
        ]
        for src, dst in (
            (slope_up_hbm, slope_up),
            (slope_gate_hbm, slope_gate),
            (normed_hbm, normed),
            (hidden_hbm, hidden),
        ):
            waits.append(load(src.at[at], dst.at[at]))
        if narrow:
            waits.append(load(column_hbm.at[at], column.at[at]))
        parts.append(waits)
    down_load.start()
    for copy in parts[0]:
        copy.start()
    block = column.shape[1]
    for h in range(2):
        for copy in parts[h]:
            copy.wait()
        if h == 0:
            down_load.wait()
            for copy in parts[1]:
                copy.start()
        at = slice(h * half, (h + 1) * half)
        if not narrow:
            column[at, :] = cot[at, pl.ds(pl.multiple_of(place_ref[2] * block, 128), block)]
        for to in tiles(hidden.shape[1], TILE):
            d_hidden = mm(cot[at, :], down[to, :], LAST)
            d_up = (d_hidden * slope_up[at, to].astype(F32)).astype(BF16)
            d_gate = (d_hidden * slope_gate[at, to].astype(F32)).astype(BF16)
            gate_part = mm(normed[at, :], d_gate, FIRST) * scale
            up_part = mm(normed[at, :], d_up, FIRST) * scale
            down_part = mm(hidden[at, to], column[at, :], FIRST) * scale
            if h == 0:
                gate_out[:, to] = gate_part
                up_out[:, to] = up_part
                down_out[to, :] = down_part
            else:
                gate_out[:, to] += gate_part
                up_out[:, to] += up_part
                down_out[to, :] += down_part


def item_late(place, pieces, column, normed, hidden, slope_up, slope_gate, w_down, scale):
    count = len(pieces)
    rows, width = count * pieces[0].shape[0], pieces[0].shape[1]
    hid, block = w_down.shape[0], normed.shape[1]
    return pl.pallas_call(
        functools.partial(late_kernel, count, scale),
        in_specs=[smem()] + [hbm()] * (count + 6),
        out_specs=[vmem()] * 3,
        out_shape=[
            jax.ShapeDtypeStruct((block, hid), F32),
            jax.ShapeDtypeStruct((block, hid), F32),
            jax.ShapeDtypeStruct((hid, block), F32),
        ],
        scratch_shapes=[
            pltpu.VMEM((rows, width), BF16),
            pltpu.VMEM((rows, block), BF16),
            pltpu.VMEM((rows, block), BF16),
            pltpu.VMEM((rows, hid), BF16),
            pltpu.VMEM((rows, hid), BF16),
            pltpu.VMEM((rows, hid), BF16),
            pltpu.VMEM((hid, width), BF16),
            pltpu.SemaphoreType.DMA((count + 11,)),
        ],
        compiler_params=params(),
        cost_estimate=cost(4 * rows * width * hid + 12 * rows * block * hid, 16e6),
        name="item_late",
    )(place, *pieces, column, normed, hidden, slope_up, slope_gate, w_down)


def place_kernel(here_ref, *refs):
    slots, out = refs[:-1], refs[-1]
    rows = slots[0].shape[0]
    for k, slot in enumerate(slots):
        out[pl.ds(pl.multiple_of((here_ref[0] ^ k) * rows, rows), rows), :] = slot[...]


def place_rows(here, slots):
    rows, width = slots[0].shape
    count = len(slots)
    return pl.pallas_call(
        place_kernel,
        in_specs=[smem()] + [vmem()] * count,
        out_specs=vmem(),
        out_shape=jax.ShapeDtypeStruct((count * rows, width), slots[0].dtype),
        compiler_params=params(),
        cost_estimate=cost(0, 4 * count * rows * width),
        name="place_rows",
    )(jnp.reshape(here, (1,)), *slots)


def grad_tables(n_chips, chip, core, order_a, order_b):
    first_a, first_b = order_a[0] >> 1, order_b[0] >> 1
    rels = sorted(range(n_chips), key=lambda r: (not (r & first_a), not (r & first_b), r))
    rows = [[], [], [], [], [], [], []]
    places = {}
    for name, first, row in (("a", first_a, 0), ("b", first_b, 3)):
        sent_order = [r for r in rels if r & first]
        kept_order = [r for r in rels if not r & first]
        last_sent = last_kept = 0
        for r in rels:
            is_sent = bool(r & first)
            if is_sent:
                last_sent = sent_order.index(r)
            else:
                last_kept = kept_order.index(r)
            rows[row].append(last_sent)
            rows[row + 1].append(last_kept)
            rows[row + 2].append(int(is_sent))
        places[name] = kept_order
    rel = jnp.array(rels, jnp.int32)
    fixed = [jnp.array(r, jnp.int32) for r in rows[:6]]
    table = jnp.stack([(chip ^ rel) * 2 + core, *fixed, rel])
    return table, places


def first_sums(got, kept, slots):
    return {r: kept[i].astype(F32) + got[i].astype(F32) for i, r in enumerate(slots)}


def sent_away(total, bit):
    away = sorted(r for r in total if r & (bit >> 1))
    return jnp.stack([total[r].astype(BF16) for r in away])


def next_sums(total, got, bit):
    away = sorted(r for r in total if r & (bit >> 1))
    return {r ^ (bit >> 1): total[r ^ (bit >> 1)] + got[i].astype(F32) for i, r in enumerate(away)}


def body(
    user_input,
    out_grad,
    hist_len,
    hist_items,
    item_row,
    item_feat,
    user_gain,
    user_gate,
    user_up,
    user_down,
    item_gain,
    item_gate,
    item_up,
    item_down,
):
    n_wide, n_narrow = lax.axis_size("wide"), lax.axis_size("narrow")
    me, here = lax.axis_index("wide"), lax.axis_index("narrow")
    chip, core = me // 2, me % 2
    n_chips = n_wide // 2
    bits = [1 << k for k in range(1, n_wide.bit_length() - 1)]
    order_a = bits
    order_b = bits[len(bits) // 2 :] + bits[: len(bits) // 2]
    user_count, hist_length, width = user_input.shape
    rows = user_count * hist_length
    item_dev = item_feat.shape[0]
    hid = user_gate.shape[1]
    block = width // n_wide
    rels = jnp.arange(n_chips, dtype=jnp.int32)
    place = jnp.stack([chip, core, me])

    def near(value):
        return [value] + [swap(value, r << 1) for r in range(1, n_chips)]

    def gather_wide(value):
        pieces = near(value)
        return pieces + [swap(piece, 1) for piece in pieces]

    feats = gather_wide(item_feat)

    normed, masked, hidden, d_gate, d_up, sent, kept = user_layer(
        place,
        hist_len,
        user_input.reshape(rows, width),
        out_grad.reshape(rows, width),
        hist_items,
        item_row,
        user_gain,
        user_gate,
        user_up,
        user_down,
        1.0 / n_narrow,
        item_dev,
    )
    sent, *_ = lax.optimization_barrier((sent, feats[1], feats[2 % n_wide]))
    got = swap(sent, 1)
    sent_table = jnp.stack([(chip ^ rels) * 2 + 1 - core])
    grads_sent = sent_grads(sent_table, normed, masked, d_gate, d_up, hidden, block)
    got, grads_sent = lax.optimization_barrier((got, grads_sent))
    grads_got = swap(grads_sent, 1)
    sums = []
    for r in range(n_chips):
        at = slice(r * item_dev, (r + 1) * item_dev)
        sums.append(kept[at].astype(F32) + got[at].astype(F32))
    pieces = [swap(sums[r].astype(BF16), r << 1) for r in range(1, n_chips)]

    group = min(8, n_wide)
    forwards = [
        item_forward(place, item_gain, feats[k : k + group], item_gate, item_up, block)
        for k in range(0, n_wide, group)
    ]

    kept_table, places = grad_tables(n_chips, chip, core, order_a, order_b)
    grads_got, _ = lax.optimization_barrier((grads_got, forwards[-1][0]))
    sent_a, kept_a, sent_b, kept_b = kept_grads(
        kept_table, normed, masked, d_gate, d_up, hidden, grads_got, block
    )
    pieces[0], sent_a, sent_b = lax.optimization_barrier((pieces[0], sent_a, sent_b))
    mine = functools.reduce(jnp.add, [p.astype(F32) for p in pieces], sums[0]).astype(BF16)
    sent_a, sent_b, mine = lax.optimization_barrier((sent_a, sent_b, mine))

    got_a, got_b = swap(sent_a, order_a[0]), swap(sent_b, order_b[0])

    quarter = item_dev // n_narrow

    def narrow_scatter(value):
        parts = lax.all_to_all(
            value.reshape(n_narrow, quarter, width), "narrow", split_axis=0, concat_axis=0, tiled=True
        )
        return jnp.sum(parts.astype(F32), axis=0)

    def narrow_slots(piece):
        return [piece] + [
            lax.ppermute(piece, "narrow", [(i, i ^ k) for i in range(n_narrow)])
            for k in range(1, n_narrow)
        ]

    def narrow_gather(piece):
        return place_rows(here, narrow_slots(piece))

    item_in = narrow_scatter(mine)
    item_cot = narrow_gather(item_in.astype(BF16))
    cots = near(item_cot)
    item_part = item_own(
        item_cot, forwards[0][2], forwards[0][3], item_gate, item_up, item_down
    )
    item_dn = narrow_scatter(item_part)

    got_a, got_b, _ = lax.optimization_barrier((got_a, got_b, item_part))
    total_a = first_sums(got_a, kept_a, places["a"])
    total_b = first_sums(got_b, kept_b, places["b"])
    for a, b in zip(order_a[1:], order_b[1:]):
        away_a, away_b = sent_away(total_a, a), sent_away(total_b, b)
        away_a, away_b, cots[-1] = lax.optimization_barrier((away_a, away_b, cots[-1]))
        got_a, got_b = swap(away_a, a), swap(away_b, b)
        if a != order_a[-1]:
            total_a, total_b = next_sums(total_a, got_a, a), next_sums(total_b, got_b, b)
    cots = cots + [swap(piece, 1) for piece in cots]

    item_scaled = item_gain.astype(F32)[None, :] * item_dn
    own = lax.dynamic_slice_in_dim(item_feat, here * quarter, quarter, axis=0).astype(F32)
    own_inv = lax.rsqrt(jnp.mean(own * own, axis=1, keepdims=True) + 1e-05)
    own_unit = own * own_inv
    item_mean = jnp.mean(item_scaled * own_unit, axis=1, keepdims=True)
    feat_rows = (item_in + own_inv * (item_scaled - own_unit * item_mean)).astype(BF16)
    feat_slots = narrow_slots(feat_rows)

    item_grads = None
    for k, (normed_k, hidden_k, slope_up_k, slope_gate_k) in enumerate(forwards):
        parts = cots[k * group : (k + 1) * group]
        column = parts[0]
        if block % 128:
            normed_k = lax.dynamic_slice_in_dim(normed_k, me * block, block, axis=1)
            column = jnp.concatenate(
                [lax.dynamic_slice_in_dim(p, me * block, block, axis=1) for p in parts], axis=0
            )
        found = item_late(
            place, parts, column, normed_k, hidden_k, slope_up_k, slope_gate_k, item_down, 1.0 / n_wide
        )
        item_grads = list(found) if item_grads is None else [a + b for a, b in zip(item_grads, found)]

    got_a, got_b, item_grads[0], *feat_slots = lax.optimization_barrier(
        (got_a, got_b, item_grads[0], *feat_slots)
    )
    feat_grad = place_rows(here, feat_slots)
    if len(order_a) > 1:
        total_a, total_b = next_sums(total_a, got_a, order_a[-1]), next_sums(total_b, got_b, order_b[-1])
    user_grads = jnp.concatenate([total_a[0], total_b[0]], axis=0) * (1.0 / n_wide)
    return (
        feat_grad,
        user_grads[:, :hid],
        user_grads[:, hid : 2 * hid],
        user_grads[:, 2 * hid :].T,
        *item_grads,
    )


def solution(mesh):
    placed = (
        P("wide", None, None),
        P("wide", None, None),
        P("wide"),
        P("wide", None),
        P(),
        P("wide", None),
        P(),
        P(None, "narrow"),
        P(None, "narrow"),
        P("narrow", None),
        P(),
        P(None, "narrow"),
        P(None, "narrow"),
        P("narrow", None),
    )
    return jax.shard_map(
        body,
        mesh=mesh,
        in_specs=placed,
        out_specs=(
            P("wide", None),
            P("wide", "narrow"),
            P("wide", "narrow"),
            P("narrow", "wide"),
            P("wide", "narrow"),
            P("wide", "narrow"),
            P("narrow", "wide"),
        ),
        check_vma=False,
    )
```

```python
import functools

import jax
import jax.numpy as jnp
from jax import lax
from jax.experimental import pallas as pl
from jax.experimental.pallas import tpu as pltpu
from jax.sharding import PartitionSpec as P

F32 = jnp.float32
BF16 = jnp.bfloat16
LAST = (((1,), (1,)), ((), ()))
FIRST = (((0,), (0,)), ((), ()))
PLAIN = (((1,), (0,)), ((), ()))
TILE = 256


def mm(a, b, dims=PLAIN):
    return lax.dot_general(a, b, dims, preferred_element_type=F32)


def params():
    return pltpu.CompilerParams(vmem_limit_bytes=60 << 20)


def cost(flops, touched):
    return pl.CostEstimate(flops=int(flops) // 6, bytes_accessed=int(touched) // 6, transcendentals=0)


def hbm():
    return pl.BlockSpec(memory_space=pl.ANY)


def vmem():
    return pl.BlockSpec(memory_space=pltpu.VMEM)


def smem():
    return pl.BlockSpec(memory_space=pltpu.SMEM)


def whole_spec(shape):
    return pl.BlockSpec(shape, lambda *_: (0,) * len(shape))


def swap(value, bit):
    count = lax.axis_size("wide")
    return lax.ppermute(value, "wide", [(i, i ^ bit) for i in range(count)])


def after(value, *others):
    return lax.optimization_barrier((value, *others))[0]


def tiles(total, size):
    size = min(size, total)
    return [slice(k, k + size) for k in range(0, total, size)]


def segment_picks(place, parity, targets, item_dev, count):
    column = lax.broadcasted_iota(jnp.int32, (1, count), 1)
    block = (place ^ (column // item_dev)) * 2 + parity
    return (targets == block * item_dev + column % item_dev).astype(BF16)


def user_kernel(
    share, item_dev, place_ref, hist_len_ref, x_hbm, og_hbm, hist_ref, item_row_ref, gain_ref,
    gate_hbm, up_hbm, down_hbm,
    normed_out, masked_out, hidden_out, d_gate_out, d_up_out, sent_out, kept_out,
    x, og, gate, up, down, normed, hidden, d_gate, d_up, gate_act, up_act, total, sent, kept, inv_ref,
    sems,
):
    loads = [
        pltpu.make_async_copy(src, dst, sems.at[k])
        for k, (src, dst) in enumerate(
            ((x_hbm, x), (gate_hbm, gate), (up_hbm, up), (og_hbm, og), (down_hbm, down))
        )
    ]
    for load in loads[:2]:
        load.start()
    stores = [
        pltpu.make_async_copy(src, dst, sems.at[5 + k])
        for k, (src, dst) in enumerate(
            (
                (normed, normed_out),
                (og, masked_out),
                (hidden, hidden_out),
                (d_gate, d_gate_out),
                (d_up, d_up_out),
            )
        )
    ]
    rows, width = x.shape
    users, length = hist_ref.shape
    hid = hidden.shape[1]
    gain = gain_ref[...].reshape(1, width).astype(F32)

    square = (length, length)
    diagonal = lax.broadcasted_iota(jnp.int32, square, 0) == lax.broadcasted_iota(jnp.int32, square, 1)
    item_row = item_row_ref[...].reshape(1, -1)
    ids = lax.broadcasted_iota(jnp.int32, (1, item_row.shape[1]), 1)
    targets = []
    for u in range(users):
        items = jnp.sum(jnp.where(diagonal, hist_ref[u : u + 1, :], 0), axis=1, keepdims=True)
        targets.append(jnp.sum(jnp.where(items == ids, item_row, 0), axis=1, keepdims=True))
    targets = jnp.concatenate(targets, axis=0)

    loads[0].wait()
    for load in loads[2:]:
        load.start()
    for at in tiles(rows, 64):
        part = x[at, :].astype(F32)
        inv = lax.rsqrt(jnp.mean(part * part, axis=1, keepdims=True) + 1e-05)
        inv_ref[at, :] = inv
        normed[at, :] = (part * inv * gain).astype(BF16)
    stores[0].start()
    loads[1].wait()
    for at in tiles(hid, TILE):
        gate_act[:, at] = mm(normed[...], gate[:, at])
    loads[2].wait()
    for at in tiles(hid, TILE):
        up_act[:, at] = mm(normed[...], up[:, at])
    loads[3].wait()
    place = lax.broadcasted_iota(jnp.int32, (length, 1), 0)
    for u in range(users):
        at = slice(u * length, (u + 1) * length)
        og[at, :] = jnp.where(place < hist_len_ref[u], og[at, :].astype(F32), 0.0).astype(BF16)
    stores[1].start()
    loads[4].wait()
    for at in tiles(hid, TILE):
        d_hidden = mm(og[...], down[at, :], LAST)
        gate_part, up_part = gate_act[:, at], up_act[:, at]
        sig = 1.0 / (1.0 + jnp.exp(-gate_part))
        silu = gate_part * sig
        hidden[:, at] = (silu * up_part).astype(BF16)
        d_up[:, at] = (d_hidden * silu).astype(BF16)
        d_gate[:, at] = (d_hidden * up_part * sig * (1.0 + gate_part * (1.0 - sig))).astype(BF16)
    for k in (2, 3, 4):
        stores[k].start()
    mean = jnp.zeros((rows, 1), F32)
    inv = inv_ref[...]
    for at in tiles(width, 512):
        part = mm(d_gate[...], gate[at, :], LAST) + mm(d_up[...], up[at, :], LAST)
        part = part * gain[:, at]
        total[:, at] = part
        mean = mean + jnp.sum(part * (x[:, at].astype(F32) * inv), axis=1, keepdims=True)
    slope = inv * inv * mean * (1.0 / width)
    chip, core = place_ref[0], place_ref[1]
    half = sent.shape[0]
    picks_sent = segment_picks(chip, 1 - core, targets, item_dev, half)
    picks_kept = segment_picks(chip, core, targets, item_dev, half)
    for at in tiles(width, 512):
        occ = (
            og[:, at].astype(F32) * share + inv * total[:, at] - x[:, at].astype(F32) * slope
        ).astype(BF16)
        sent[:, at] = mm(picks_sent, occ, FIRST).astype(BF16)
        kept[:, at] = mm(picks_kept, occ, FIRST).astype(BF16)
        for src, dst in ((sent, sent_out), (kept, kept_out)):
            stores.append(pltpu.make_async_copy(src.at[:, at], dst.at[:, at], sems.at[5 + len(stores)]))
            stores[-1].start()
    for store in stores:
        store.wait()


def user_layer(place, hist_len, x, og, hist, item_row, gain, w_gate, w_up, w_down, share, item_dev):
    rows, width = x.shape
    hid = w_gate.shape[1]
    half = item_row.shape[0] // 2
    wide = jax.ShapeDtypeStruct((rows, width), BF16)
    narrow = jax.ShapeDtypeStruct((rows, hid), BF16)
    summed = jax.ShapeDtypeStruct((half, width), BF16)
    return pl.pallas_call(
        functools.partial(user_kernel, share, item_dev),
        in_specs=[smem()] * 2 + [hbm()] * 2 + [vmem()] * 3 + [hbm()] * 3,
        out_specs=[hbm()] * 7,
        out_shape=[wide, wide, narrow, narrow, narrow, summed, summed],
        scratch_shapes=[
            pltpu.VMEM((rows, width), BF16),
            pltpu.VMEM((rows, width), BF16),
            pltpu.VMEM((width, hid), BF16),
            pltpu.VMEM((width, hid), BF16),
            pltpu.VMEM((hid, width), BF16),
            pltpu.VMEM((rows, width), BF16),
            pltpu.VMEM((rows, hid), BF16),
            pltpu.VMEM((rows, hid), BF16),
            pltpu.VMEM((rows, hid), BF16),
            pltpu.VMEM((rows, hid), F32),
            pltpu.VMEM((rows, hid), F32),
            pltpu.VMEM((rows, width), F32),
            pltpu.VMEM((half, width), BF16),
            pltpu.VMEM((half, width), BF16),
            pltpu.VMEM((rows, 1), F32),
            pltpu.SemaphoreType.DMA((10 + 2 * len(tiles(width, 512)),)),
        ],
        compiler_params=params(),
        cost_estimate=cost(10 * rows * width * hid, 24e6),
        name="user_layer",
    )(place, hist_len, x, og, hist, item_row, gain, w_gate, w_up, w_down)


def grad_rows(normed_ref, masked_ref, d_gate_ref, d_up_ref, hidden_ref):
    left, right = normed_ref[...], masked_ref[...]
    return (
        mm(left, d_gate_ref[...], FIRST),
        mm(left, d_up_ref[...], FIRST),
        mm(right, hidden_ref[...], FIRST),
    )


def sent_kernel(table_ref, normed_ref, masked_ref, d_gate_ref, d_up_ref, hidden_ref, out_ref):
    hid = hidden_ref.shape[1]
    found = grad_rows(normed_ref, masked_ref, d_gate_ref, d_up_ref, hidden_ref)
    for k, piece in enumerate(found):
        out_ref[0, :, k * hid : (k + 1) * hid] = piece.astype(BF16)


def kept_kernel(
    table_ref, normed_ref, masked_ref, d_gate_ref, d_up_ref, hidden_ref, got_ref,
    sent_a, kept_a, sent_b, kept_b,
):
    step = pl.program_id(0)
    hid = hidden_ref.shape[1]
    cut = got_ref.shape[1] // 2
    found = grad_rows(normed_ref, masked_ref, d_gate_ref, d_up_ref, hidden_ref)
    for first, sent, kept, flag in ((0, sent_a, kept_a, 3), (cut, sent_b, kept_b, 6)):
        for k, piece in enumerate(found):
            at = slice(k * hid, (k + 1) * hid)
            value = piece[first : first + cut] + got_ref[0, first : first + cut, at].astype(F32)
            value = value.astype(BF16)

            @pl.when(table_ref[flag, step] == 1)
            def _(sent=sent, value=value, at=at):
                sent[0, :, at] = value

            @pl.when(table_ref[flag, step] == 0)
            def _(kept=kept, value=value, at=at):
                kept[0, :, at] = value


def lhs_specs(rows, block, hid):
    if block % 128:
        column = pl.BlockSpec((None, rows, block), lambda s, t: (s, 0, 0))
    else:
        column = pl.BlockSpec((rows, block), lambda s, t: (0, t[0, s]))
    return [column, column] + [whole_spec((rows, hid))] * 3


def lhs_arrays(table, normed, masked, block):
    if block % 128 == 0:
        return normed, masked
    return tuple(
        jnp.take(jnp.swapaxes(a.reshape(a.shape[0], -1, block), 0, 1), table[0], axis=0)
        for a in (normed, masked)
    )


def sent_grads(table, normed, masked, d_gate, d_up, hidden, block):
    rows, hid = hidden.shape
    count = table.shape[1]
    return pl.pallas_call(
        sent_kernel,
        grid_spec=pltpu.PrefetchScalarGridSpec(
            num_scalar_prefetch=1,
            grid=(count,),
            in_specs=lhs_specs(rows, block, hid),
            out_specs=pl.BlockSpec((1, block, 3 * hid), lambda s, t: (s, 0, 0)),
        ),
        out_shape=jax.ShapeDtypeStruct((count, block, 3 * hid), BF16),
        compiler_params=params(),
        cost_estimate=cost(6 * rows * block * count * hid, 10e6),
        name="sent_grads",
    )(table, *lhs_arrays(table, normed, masked, block), d_gate, d_up, hidden)


def kept_grads(table, normed, masked, d_gate, d_up, hidden, got, block):
    rows, hid = hidden.shape
    count = table.shape[1]
    piece = jax.ShapeDtypeStruct((count // 2, block // 2, 3 * hid), BF16)

    def out(row):
        return pl.BlockSpec((1, block // 2, 3 * hid), lambda s, t: (t[row, s], 0, 0))

    return pl.pallas_call(
        kept_kernel,
        grid_spec=pltpu.PrefetchScalarGridSpec(
            num_scalar_prefetch=1,
            grid=(count,),
            in_specs=lhs_specs(rows, block, hid)
            + [pl.BlockSpec((1, block, 3 * hid), lambda s, t: (t[7, s], 0, 0))],
            out_specs=[out(1), out(2), out(4), out(5)],
        ),
        out_shape=[piece] * 4,
        compiler_params=params(),
        cost_estimate=cost(6 * rows * block * count * hid, 15e6),
        name="kept_grads",
    )(table, *lhs_arrays(table, normed, masked, block), d_gate, d_up, hidden, got)


def forward_kernel(count, place_ref, gain_ref, *refs):
    feats, (gate_hbm, up_hbm) = refs[:count], refs[count : count + 2]
    normed_out, hidden_out, slope_up_out, slope_gate_out = refs[count + 2 : count + 6]
    x, normed, gate, up, gate_act, hidden, slope_up, slope_gate, sems = refs[count + 6 :]
    width, hid = gate.shape
    all_rows = x.shape[0]
    rows = all_rows // count
    pieces = [
        pltpu.make_async_copy(feats[k], x.at[pl.ds(k * rows, rows)], sems.at[k]) for k in range(count)
    ]
    gate_load = pltpu.make_async_copy(gate_hbm, gate, sems.at[count])
    up_load = pltpu.make_async_copy(up_hbm, up, sems.at[count + 1])
    halves = [range(count // 2), range(count // 2, count)]
    for k in halves[0]:
        pieces[k].start()
    gate_load.start()
    gain = gain_ref[...].reshape(1, width).astype(F32)

    def normalise(k):
        for at in tiles(rows, 64):
            at = slice(k * rows + at.start, k * rows + at.stop)
            part = x[at, :].astype(F32)
            inv = lax.rsqrt(jnp.mean(part * part, axis=1, keepdims=True) + 1e-05)
            normed[at, :] = (part * inv * gain).astype(BF16)

    for k in halves[0]:
        pieces[k].wait()
    for k in halves[1]:
        pieces[k].start()
    up_load.start()
    for k in halves[0]:
        normalise(k)
    gate_load.wait()
    for h in range(2):
        part = slice(h * all_rows // 2, (h + 1) * all_rows // 2)
        if h == 1:
            for k in halves[1]:
                pieces[k].wait()
            for k in halves[1]:
                normalise(k)
        for at in tiles(hid, TILE):
            gate_act[part, at] = mm(normed[part, :], gate[:, at])
    block = normed_out.shape[1]
    mine = normed
    if block < width:
        mine = normed.at[:, pl.ds(pl.multiple_of(place_ref[2] * block, 128), block)]
    stores = [pltpu.make_async_copy(mine, normed_out, sems.at[count + 2])]
    stores[0].start()
    up_load.wait()
    for at in tiles(hid, TILE):
        up_part = mm(normed[...], up[:, at])
        gate_part = gate_act[:, at]
        sig = 1.0 / (1.0 + jnp.exp(-gate_part))
        silu = gate_part * sig
        hidden[:, at] = (silu * up_part).astype(BF16)
        slope_up[:, at] = silu.astype(BF16)
        slope_gate[:, at] = (up_part * sig * (1.0 + gate_part * (1.0 - sig))).astype(BF16)
        for src, dst in ((hidden, hidden_out), (slope_up, slope_up_out), (slope_gate, slope_gate_out)):
            sem = sems.at[count + 2 + len(stores)]
            stores.append(pltpu.make_async_copy(src.at[:, at], dst.at[:, at], sem))
            stores[-1].start()
    for store in stores:
        store.wait()


def item_forward(place, gain, feats, w_gate, w_up, block):
    count = len(feats)
    rows, width = count * feats[0].shape[0], feats[0].shape[1]
    hid = w_gate.shape[1]
    kept = width if block % 128 else block
    narrow = jax.ShapeDtypeStruct((rows, hid), BF16)
    return pl.pallas_call(
        functools.partial(forward_kernel, count),
        in_specs=[smem(), vmem()] + [hbm()] * (count + 2),
        out_specs=[hbm()] * 4,
        out_shape=[jax.ShapeDtypeStruct((rows, kept), BF16)] + [narrow] * 3,
        scratch_shapes=[
            pltpu.VMEM((rows, width), BF16),
            pltpu.VMEM((rows, width), BF16),
            pltpu.VMEM((width, hid), BF16),
            pltpu.VMEM((width, hid), BF16),
            pltpu.VMEM((rows, hid), F32),
            pltpu.VMEM((rows, hid), BF16),
            pltpu.VMEM((rows, hid), BF16),
            pltpu.VMEM((rows, hid), BF16),
            pltpu.SemaphoreType.DMA((count + 3 + 3 * len(tiles(hid, TILE)),)),
        ],
        compiler_params=params(),
        cost_estimate=cost(4 * rows * width * hid, 16e6),
        name="item_forward",
    )(place, gain, *feats, w_gate, w_up)


def own_kernel(here_ref, cot, slope_up, slope_gate, gate_hbm, up_hbm, down_hbm, *refs):
    outs, (total, gate, up, down, sems) = refs[:-5], refs[-5:]
    loads = [
        pltpu.make_async_copy(src, dst, sems.at[k])
        for k, (src, dst) in enumerate(((down_hbm, down), (gate_hbm, gate), (up_hbm, up)))
    ]
    for load in loads:
        load.start()
    loads[0].wait()
    d_hidden = mm(cot[...], down[...], LAST)
    d_up = (d_hidden * slope_up[...].astype(F32)).astype(BF16)
    d_gate = (d_hidden * slope_gate[...].astype(F32)).astype(BF16)
    loads[1].wait()
    loads[2].wait()
    for at in tiles(total.shape[1], 512):
        total[:, at] = (mm(d_gate, gate[at, :], LAST) + mm(d_up, up[at, :], LAST)).astype(BF16)
    cut_rows(here_ref[0], total, outs)


def item_own(here, cot, slope_up, slope_gate, w_gate, w_up, w_down, n_narrow):
    rows, width = cot.shape
    hid = w_gate.shape[1]
    part = (rows // n_narrow, width)
    return pl.pallas_call(
        own_kernel,
        grid=(1,),
        in_specs=[smem(), whole_spec((rows, width)), whole_spec((rows, hid)), whole_spec((rows, hid))]
        + [hbm()] * 3,
        out_specs=[whole_spec(part)] * n_narrow,
        out_shape=[jax.ShapeDtypeStruct(part, BF16)] * n_narrow,
        scratch_shapes=[
            pltpu.VMEM((rows, width), BF16),
            pltpu.VMEM((width, hid), BF16),
            pltpu.VMEM((width, hid), BF16),
            pltpu.VMEM((hid, width), BF16),
            pltpu.SemaphoreType.DMA((3,)),
        ],
        compiler_params=params(),
        cost_estimate=cost(6 * rows * width * hid, 11e6),
        name="item_own",
    )(jnp.reshape(here, (1,)), cot, slope_up, slope_gate, w_gate, w_up, w_down)


def late_kernel(slots, before, scale, place_ref, *refs):
    count = len(slots)
    pieces, (column_hbm, normed_hbm, hidden_hbm, slope_up_hbm, slope_gate_hbm, down_hbm) = (
        refs[:count],
        refs[count : count + 6],
    )
    earlier, refs = (refs[count + 6 : count + 9], refs[count + 9 :]) if before else (None, refs[count + 6 :])
    outs, (cot, column, normed, hidden, slope_up, slope_gate, down, sems) = refs[:3], refs[3:]
    rows = cot.shape[0] // count
    block = column.shape[1]
    narrow = block % 128 != 0
    hid = hidden.shape[1]
    copies = [(piece, cot.at[pl.ds(k * rows, rows)]) for k, piece in enumerate(pieces)]
    copies += [(down_hbm.at[to], down.at[to]) for to in tiles(hid, TILE)]
    for k, slot in enumerate(slots):
        at, to = pl.ds(slot * rows, rows), pl.ds(k * rows, rows)
        copies += [(slope_up_hbm.at[at], slope_up.at[to]), (slope_gate_hbm.at[at], slope_gate.at[to])]
        copies += [(normed_hbm.at[at], normed.at[to]), (hidden_hbm.at[at], hidden.at[to])]
    if narrow:
        copies.append((column_hbm, column))
    loads = [pltpu.make_async_copy(src, dst, sems.at[k]) for k, (src, dst) in enumerate(copies)]
    for load in loads:
        load.start()
    for load in loads[:count]:
        load.wait()
    if not narrow:
        column[...] = cot[:, pl.ds(pl.multiple_of(place_ref[2] * block, 128), block)]
    downs, rest = loads[count : count + len(tiles(hid, TILE))], loads[count + len(tiles(hid, TILE)) :]
    for k, to in enumerate(tiles(hid, TILE)):
        downs[k].wait()
        d_hidden = mm(cot[...], down[to, :], LAST)
        if k == 0:
            for load in rest:
                load.wait()
        d_up = (d_hidden * slope_up[:, to].astype(F32)).astype(BF16)
        d_gate = (d_hidden * slope_gate[:, to].astype(F32)).astype(BF16)
        gate_part = mm(normed[...], d_gate, FIRST) * scale
        up_part = mm(normed[...], d_up, FIRST) * scale
        down_part = mm(hidden[:, to], column[...], FIRST) * scale
        if before:
            gate_part += earlier[0][:, to]
            up_part += earlier[1][:, to]
            down_part += earlier[2][to, :]
        outs[0][:, to] = gate_part
        outs[1][:, to] = up_part
        outs[2][to, :] = down_part


def item_late(place, slots, pieces, column, normed, hidden, slope_up, slope_gate, w_down, before, scale):
    count = len(pieces)
    rows, width = count * pieces[0].shape[0], pieces[0].shape[1]
    hid, block = w_down.shape[0], normed.shape[1]
    before = list(before) if before is not None else []
    return pl.pallas_call(
        functools.partial(late_kernel, tuple(slots), bool(before), scale),
        in_specs=[smem()] + [hbm()] * (count + 6) + [vmem()] * len(before),
        out_specs=[vmem()] * 3,
        out_shape=[
            jax.ShapeDtypeStruct((block, hid), F32),
            jax.ShapeDtypeStruct((block, hid), F32),
            jax.ShapeDtypeStruct((hid, block), F32),
        ],
        scratch_shapes=[
            pltpu.VMEM((rows, width), BF16),
            pltpu.VMEM((rows, block), BF16),
            pltpu.VMEM((rows, block), BF16),
            pltpu.VMEM((rows, hid), BF16),
            pltpu.VMEM((rows, hid), BF16),
            pltpu.VMEM((rows, hid), BF16),
            pltpu.VMEM((hid, width), BF16),
            pltpu.SemaphoreType.DMA((5 * count + 1 + len(tiles(hid, TILE)),)),
        ],
        compiler_params=params(),
        cost_estimate=cost(4 * rows * width * hid + 12 * rows * block * hid, 16e6),
        name="item_late",
    )(
        place, *pieces, column, normed, hidden, slope_up, slope_gate, w_down, *before,
    )


def merge_kernel(here_ref, kept_ref, got_ref, *refs):
    count = sum(1 for r in refs if r.shape == kept_ref.shape) - 1
    pieces, outs, total = refs[:count], refs[count:-1], refs[-1]
    value = kept_ref[...].astype(F32) + got_ref[...].astype(F32)
    for piece in pieces:
        value = value + piece[...].astype(F32)
    total[...] = value.astype(BF16)
    cut_rows(here_ref[0], total, outs)


def cut_rows(here, total, outs):
    rows = outs[0].shape[0]
    for k, out in enumerate(outs):
        out[...] = total[pl.ds(pl.multiple_of((here ^ k) * rows, rows), rows), :]


def merge_chips(here, kept, got, pieces, n_narrow):
    rows, width = pieces[0].shape
    spec = whole_spec((rows, width))
    part = (rows // n_narrow, width)
    return pl.pallas_call(
        merge_kernel,
        grid=(1,),
        in_specs=[smem()] + [spec] * (2 + len(pieces)),
        out_specs=[whole_spec(part)] * n_narrow,
        out_shape=[jax.ShapeDtypeStruct(part, BF16)] * n_narrow,
        scratch_shapes=[pltpu.VMEM((rows, width), BF16)],
        compiler_params=params(),
        cost_estimate=cost(0, 2 * (4 + len(pieces)) * rows * width),
        name="merge_chips",
    )(jnp.reshape(here, (1,)), kept, got, *pieces)


def final_kernel(scale, here_ref, kept_a, got_a, kept_b, got_b, *refs):
    slots, (feat_out, gate_out, up_out, down_out) = refs[:-4], refs[-4:]
    cut, hid = kept_a.shape[0], gate_out.shape[1]
    for half, (kept, got) in enumerate(((kept_a, got_a), (kept_b, got_b))):
        total = (kept[...] + got[...].astype(F32)) * scale
        at = slice(half * cut, (half + 1) * cut)
        gate_out[at, :] = total[:, :hid]
        up_out[at, :] = total[:, hid : 2 * hid]
        down_out[:, at] = total[:, 2 * hid :].T
    rows = slots[0].shape[0]
    for k, slot in enumerate(slots):
        feat_out[pl.ds(pl.multiple_of((here_ref[0] ^ k) * rows, rows), rows), :] = slot[...]


def final_sums(here, kept_a, got_a, kept_b, got_b, slots, scale):
    cut, hid = kept_a.shape[0], kept_a.shape[1] // 3
    rows, width = slots[0].shape
    return pl.pallas_call(
        functools.partial(final_kernel, scale),
        in_specs=[smem()] + [vmem()] * (4 + len(slots)),
        out_specs=[vmem()] * 4,
        out_shape=[
            jax.ShapeDtypeStruct((len(slots) * rows, width), BF16),
            jax.ShapeDtypeStruct((2 * cut, hid), F32),
            jax.ShapeDtypeStruct((2 * cut, hid), F32),
            jax.ShapeDtypeStruct((hid, 2 * cut), F32),
        ],
        compiler_params=params(),
        cost_estimate=cost(0, 30 * cut * hid),
        name="final_sums",
    )(jnp.reshape(here, (1,)), kept_a, got_a, kept_b, got_b, *slots)


def place_kernel(here_ref, *refs):
    slots, out = refs[:-1], refs[-1]
    rows = slots[0].shape[0]
    for k, slot in enumerate(slots):
        out[pl.ds(pl.multiple_of((here_ref[0] ^ k) * rows, rows), rows), :] = slot[...]


def place_rows(here, slots):
    rows, width = slots[0].shape
    count = len(slots)
    return pl.pallas_call(
        place_kernel,
        in_specs=[smem()] + [vmem()] * count,
        out_specs=vmem(),
        out_shape=jax.ShapeDtypeStruct((count * rows, width), slots[0].dtype),
        compiler_params=params(),
        cost_estimate=cost(0, 4 * count * rows * width),
        name="place_rows",
    )(jnp.reshape(here, (1,)), *slots)


def grad_tables(n_chips, chip, core, order_a, order_b):
    first_a, first_b = order_a[0] >> 1, order_b[0] >> 1
    rels = sorted(range(n_chips), key=lambda r: (not (r & first_a), not (r & first_b), r))
    rows = [[], [], [], [], [], [], []]
    places = {}
    for name, first, row in (("a", first_a, 0), ("b", first_b, 3)):
        sent_order = [r for r in rels if r & first]
        kept_order = [r for r in rels if not r & first]
        last_sent = last_kept = 0
        for r in rels:
            is_sent = bool(r & first)
            if is_sent:
                last_sent = sent_order.index(r)
            else:
                last_kept = kept_order.index(r)
            rows[row].append(last_sent)
            rows[row + 1].append(last_kept)
            rows[row + 2].append(int(is_sent))
        places[name] = kept_order
    rel = jnp.array(rels, jnp.int32)
    fixed = [jnp.array(r, jnp.int32) for r in rows[:6]]
    table = jnp.stack([(chip ^ rel) * 2 + core, *fixed, rel])
    return table, places


def first_sums(got, kept, slots):
    return {r: kept[i].astype(F32) + got[i].astype(F32) for i, r in enumerate(slots)}


def sent_away(total, bit):
    away = sorted(r for r in total if r & (bit >> 1))
    return jnp.stack([total[r].astype(BF16) for r in away])


def next_sums(total, got, bit):
    away = sorted(r for r in total if r & (bit >> 1))
    return {r ^ (bit >> 1): total[r ^ (bit >> 1)] + got[i].astype(F32) for i, r in enumerate(away)}


def body(
    user_input,
    out_grad,
    hist_len,
    hist_items,
    item_row,
    item_feat,
    user_gain,
    user_gate,
    user_up,
    user_down,
    item_gain,
    item_gate,
    item_up,
    item_down,
):
    n_wide, n_narrow = lax.axis_size("wide"), lax.axis_size("narrow")
    me, here = lax.axis_index("wide"), lax.axis_index("narrow")
    chip, core = me // 2, me % 2
    n_chips = n_wide // 2
    bits = [1 << k for k in range(1, n_wide.bit_length() - 1)]
    order_a = bits
    order_b = bits[len(bits) // 2 :] + bits[: len(bits) // 2]
    user_count, hist_length, width = user_input.shape
    rows = user_count * hist_length
    item_dev = item_feat.shape[0]
    hid = user_gate.shape[1]
    block = width // n_wide
    rels = jnp.arange(n_chips, dtype=jnp.int32)
    place = jnp.stack([chip, core, me])

    def near(value):
        return [value] + [swap(value, r << 1) for r in range(1, n_chips)]

    def gather_wide(value):
        pieces = near(value)
        return pieces + [swap(piece, 1) for piece in pieces]

    feats = gather_wide(item_feat)

    normed, masked, hidden, d_gate, d_up, sent, kept = user_layer(
        place,
        hist_len,
        user_input.reshape(rows, width),
        out_grad.reshape(rows, width),
        hist_items,
        item_row,
        user_gain,
        user_gate,
        user_up,
        user_down,
        1.0 / n_narrow,
        item_dev,
    )
    sent, *_ = lax.optimization_barrier((sent, *feats[1:n_chips]))
    got = swap(sent, 1)
    sent_table = jnp.stack([(chip ^ rels) * 2 + 1 - core])
    grads_sent = sent_grads(sent_table, normed, masked, d_gate, d_up, hidden, block)
    got, grads_sent = lax.optimization_barrier((got, grads_sent))
    grads_got = swap(grads_sent, 1)
    sums = []
    for r in range(1, n_chips):
        at = slice(r * item_dev, (r + 1) * item_dev)
        sums.append((kept[at].astype(F32) + got[at].astype(F32)).astype(BF16))
    pieces = [swap(total, r << 1) for r, total in enumerate(sums, 1)]

    group = min(8, n_wide)
    forwards = [
        item_forward(place, item_gain, feats[k : k + group], item_gate, item_up, block)
        for k in range(0, n_wide, group)
    ]

    kept_table, places = grad_tables(n_chips, chip, core, order_a, order_b)
    grads_got, _ = lax.optimization_barrier((grads_got, forwards[-1][0]))
    sent_a, kept_a, sent_b, kept_b = kept_grads(
        kept_table, normed, masked, d_gate, d_up, hidden, grads_got, block
    )
    pieces[0], sent_a, sent_b = lax.optimization_barrier((pieces[0], sent_a, sent_b))
    mine = list(merge_chips(here, kept, got, pieces, n_narrow))
    sent_a, sent_b, mine[0] = lax.optimization_barrier((sent_a, sent_b, mine[0]))
    got_a, got_b = swap(sent_a, order_a[0]), swap(sent_b, order_b[0])

    quarter = item_dev // n_narrow

    def narrow_scatter(parts):
        got = [
            part if k == 0 else lax.ppermute(part, "narrow", [(i, i ^ k) for i in range(n_narrow)])
            for k, part in enumerate(parts)
        ]
        return functools.reduce(jnp.add, [part.astype(F32) for part in got])

    def narrow_slots(piece):
        return [piece] + [
            lax.ppermute(piece, "narrow", [(i, i ^ k) for i in range(n_narrow)])
            for k in range(1, n_narrow)
        ]

    def narrow_gather(piece):
        return place_rows(here, narrow_slots(piece))

    item_in = narrow_scatter(mine)
    item_cot = narrow_gather(item_in.astype(BF16))
    cots = [item_cot] + [swap(item_cot, r << 1) for r in range(1, n_chips - 1)]
    last_cot, *cots[1:] = lax.optimization_barrier((item_cot, *cots[1:]))
    cots.append(swap(last_cot, (n_chips - 1) << 1))
    item_part = item_own(
        here, item_cot, forwards[0][2], forwards[0][3], item_gate, item_up, item_down, n_narrow
    )
    item_dn = narrow_scatter(item_part)

    got_a, got_b, _ = lax.optimization_barrier((got_a, got_b, item_part[0]))
    assert len(order_a) > 1
    total_a = first_sums(got_a, kept_a, places["a"])
    total_b = first_sums(got_b, kept_b, places["b"])
    for a, b in zip(order_a[1:], order_b[1:]):
        away_a, away_b = sent_away(total_a, a), sent_away(total_b, b)
        away_a, away_b, cots[1] = lax.optimization_barrier((away_a, away_b, cots[1]))
        got_a, got_b = swap(away_a, a), swap(away_b, b)
        if a != order_a[-1]:
            total_a, total_b = next_sums(total_a, got_a, a), next_sums(total_b, got_b, b)
    cots = cots + [swap(piece, 1) for piece in cots]

    slots = range(n_wide)
    if n_wide == group:
        arrived = [k for k in slots if k % n_chips != n_chips - 1]
        lots = [arrived, [k for k in slots if k not in arrived]]
    else:
        lots = [list(slots[k : k + group]) for k in range(0, n_wide, group)]

    def late(lot, before):
        normed_k, hidden_k, slope_up_k, slope_gate_k = forwards[lot[0] // group]
        parts = [cots[k] for k in lot]
        column = parts[0]
        if block % 128:
            normed_k = lax.dynamic_slice_in_dim(normed_k, me * block, block, axis=1)
            column = jnp.concatenate(
                [lax.dynamic_slice_in_dim(p, me * block, block, axis=1) for p in parts], axis=0
            )
        return list(
            item_late(
                place, [k % group for k in lot], parts, column, normed_k, hidden_k, slope_up_k,
                slope_gate_k, item_down, before, 1.0 / n_wide,
            )
        )

    item_grads = late(lots[0], None)
    own_feat = lax.dynamic_slice_in_dim(item_feat, here * quarter, quarter, axis=0)
    own_feat, item_in, item_grads[0] = lax.optimization_barrier((own_feat, item_in, item_grads[0]))
    item_scaled = item_gain.astype(F32)[None, :] * item_dn
    own = own_feat.astype(F32)
    own_inv = lax.rsqrt(jnp.mean(own * own, axis=1, keepdims=True) + 1e-05)
    own_unit = own * own_inv
    item_mean = jnp.mean(item_scaled * own_unit, axis=1, keepdims=True)
    feat_rows = (item_in + own_inv * (item_scaled - own_unit * item_mean)).astype(BF16)
    feat_slots = narrow_slots(feat_rows)

    for lot in lots[1:]:
        item_grads = late(lot, item_grads)

    got_a, got_b, item_grads[0], *feat_slots = lax.optimization_barrier(
        (got_a, got_b, item_grads[0], *feat_slots)
    )
    feat_grad, *user_grads = final_sums(
        here, total_a[0], got_a[0], total_b[0], got_b[0], feat_slots, 1.0 / n_wide
    )
    return (feat_grad, *user_grads, *item_grads)


def solution(mesh):
    placed = (
        P("wide", None, None),
        P("wide", None, None),
        P("wide"),
        P("wide", None),
        P(),
        P("wide", None),
        P(),
        P(None, "narrow"),
        P(None, "narrow"),
        P("narrow", None),
        P(),
        P(None, "narrow"),
        P(None, "narrow"),
        P("narrow", None),
    )
    return jax.shard_map(
        body,
        mesh=mesh,
        in_specs=placed,
        out_specs=(
            P("wide", None),
            P("wide", "narrow"),
            P("wide", "narrow"),
            P("narrow", "wide"),
            P("wide", "narrow"),
            P("wide", "narrow"),
            P("narrow", "wide"),
        ),
        check_vma=False,
    )
```

```python
import functools

import jax
import jax.numpy as jnp
import numpy as np
from jax import lax
from jax.experimental import pallas as pl
from jax.experimental.pallas import tpu as pltpu
from jax.sharding import PartitionSpec as P

F32 = jnp.float32
BF16 = jnp.bfloat16
LAST = (((1,), (1,)), ((), ()))
FIRST = (((0,), (0,)), ((), ()))
PLAIN = (((1,), (0,)), ((), ()))
TILE = 256


def mm(a, b, dims=PLAIN):
    return lax.dot_general(a, b, dims, preferred_element_type=F32)


def params():
    return pltpu.CompilerParams(vmem_limit_bytes=60 << 20)


def cost(flops, touched):
    return pl.CostEstimate(flops=int(flops) // 6, bytes_accessed=int(touched) // 6, transcendentals=0)


def hbm():
    return pl.BlockSpec(memory_space=pl.ANY)


def vmem():
    return pl.BlockSpec(memory_space=pltpu.VMEM)


def smem():
    return pl.BlockSpec(memory_space=pltpu.SMEM)


def whole_spec(shape):
    return pl.BlockSpec(shape, lambda *_: (0,) * len(shape))


def swap(value, bit):
    count = lax.axis_size("wide")
    return lax.ppermute(value, "wide", [(i, i ^ bit) for i in range(count)])


def after(value, *others):
    return lax.optimization_barrier((value, *others))[0]


def tiles(total, size):
    size = min(size, total)
    return [slice(k, k + size) for k in range(0, total, size)]


def segment_picks(place, parity, targets, item_dev, count):
    column = lax.broadcasted_iota(jnp.int32, (1, count), 1)
    block = (place ^ (column // item_dev)) * 2 + parity
    return (targets == block * item_dev + column % item_dev).astype(BF16)


def user_kernel(
    share, item_dev, place_ref, hist_len_ref, x_hbm, og_hbm, hist_ref, item_row_ref, gain_ref,
    gate_hbm, up_hbm, down_hbm,
    normed_out, masked_out, hidden_out, d_both_out, sent_out, kept_out,
    x, og, gate, up, down, normed, hidden, d_both, gate_act, up_act, total, sent, kept, inv_ref,
    sems,
):
    loads = [
        pltpu.make_async_copy(src, dst, sems.at[k])
        for k, (src, dst) in enumerate(
            ((x_hbm, x), (gate_hbm, gate), (up_hbm, up), (og_hbm, og), (down_hbm, down))
        )
    ]
    for load in loads[:2]:
        load.start()
    stores = [
        pltpu.make_async_copy(src, dst, sems.at[5 + k])
        for k, (src, dst) in enumerate(
            (
                (normed, normed_out),
                (og, masked_out),
                (hidden, hidden_out),
                (d_both, d_both_out),
            )
        )
    ]
    rows, width = x.shape
    users, length = hist_ref.shape
    hid = hidden.shape[1]
    gain = gain_ref[...].reshape(1, width).astype(F32)

    square = (length, length)
    diagonal = lax.broadcasted_iota(jnp.int32, square, 0) == lax.broadcasted_iota(jnp.int32, square, 1)
    item_row = item_row_ref[...].reshape(1, -1)
    ids = lax.broadcasted_iota(jnp.int32, (1, item_row.shape[1]), 1)
    targets = []
    for u in range(users):
        items = jnp.sum(jnp.where(diagonal, hist_ref[u : u + 1, :], 0), axis=1, keepdims=True)
        targets.append(jnp.sum(jnp.where(items == ids, item_row, 0), axis=1, keepdims=True))
    targets = jnp.concatenate(targets, axis=0)

    loads[0].wait()
    for load in loads[2:]:
        load.start()
    for at in tiles(rows, 64):
        part = x[at, :].astype(F32)
        inv = lax.rsqrt(jnp.mean(part * part, axis=1, keepdims=True) + 1e-05)
        inv_ref[at, :] = inv
        normed[at, :] = (part * inv * gain).astype(BF16)
    stores[0].start()
    loads[1].wait()
    for at in tiles(hid, TILE):
        gate_act[:, at] = mm(normed[...], gate[:, at])
    loads[2].wait()
    for at in tiles(hid, TILE):
        up_act[:, at] = mm(normed[...], up[:, at])
    loads[3].wait()
    place = lax.broadcasted_iota(jnp.int32, (length, 1), 0)
    for u in range(users):
        at = slice(u * length, (u + 1) * length)
        og[at, :] = jnp.where(place < hist_len_ref[u], og[at, :].astype(F32), 0.0).astype(BF16)
    stores[1].start()
    loads[4].wait()
    for at in tiles(hid, TILE):
        d_hidden = mm(og[...], down[at, :], LAST)
        gate_part, up_part = gate_act[:, at], up_act[:, at]
        sig = 1.0 / (1.0 + jnp.exp(-gate_part))
        silu = gate_part * sig
        hidden[:, at] = (silu * up_part).astype(BF16)
        d_both[:, hid + at.start : hid + at.stop] = (d_hidden * silu).astype(BF16)
        d_both[:, at] = (d_hidden * up_part * sig * (1.0 + gate_part * (1.0 - sig))).astype(BF16)
    for k in (2, 3):
        stores[k].start()
    mean = jnp.zeros((rows, 1), F32)
    inv = inv_ref[...]
    for at in tiles(width, 512):
        part = mm(d_both[:, :hid], gate[at, :], LAST) + mm(d_both[:, hid:], up[at, :], LAST)
        part = part * gain[:, at]
        total[:, at] = part
        mean = mean + jnp.sum(part * (x[:, at].astype(F32) * inv), axis=1, keepdims=True)
    slope = inv * inv * mean * (1.0 / width)
    chip, core = place_ref[0], place_ref[1]
    half = sent.shape[0]
    picks_sent = segment_picks(chip, 1 - core, targets, item_dev, half)
    picks_kept = segment_picks(chip, core, targets, item_dev, half)
    for at in tiles(width, 512):
        occ = (
            og[:, at].astype(F32) * share + inv * total[:, at] - x[:, at].astype(F32) * slope
        ).astype(BF16)
        sent[:, at] = mm(picks_sent, occ, FIRST).astype(BF16)
        kept[:, at] = mm(picks_kept, occ, FIRST).astype(BF16)
        for src, dst in ((sent, sent_out), (kept, kept_out)):
            stores.append(pltpu.make_async_copy(src.at[:, at], dst.at[:, at], sems.at[5 + len(stores)]))
            stores[-1].start()
    for store in stores:
        store.wait()


def user_layer(place, hist_len, x, og, hist, item_row, gain, w_gate, w_up, w_down, share, item_dev):
    rows, width = x.shape
    hid = w_gate.shape[1]
    half = item_row.shape[0] // 2
    wide = jax.ShapeDtypeStruct((rows, width), BF16)
    narrow = jax.ShapeDtypeStruct((rows, hid), BF16)
    summed = jax.ShapeDtypeStruct((half, width), BF16)
    return pl.pallas_call(
        functools.partial(user_kernel, share, item_dev),
        in_specs=[smem()] * 2 + [hbm()] * 2 + [vmem()] * 3 + [hbm()] * 3,
        out_specs=[hbm()] * 6,
        out_shape=[wide, wide, narrow, jax.ShapeDtypeStruct((rows, 2 * hid), BF16), summed, summed],
        scratch_shapes=[
            pltpu.VMEM((rows, width), BF16),
            pltpu.VMEM((rows, width), BF16),
            pltpu.VMEM((width, hid), BF16),
            pltpu.VMEM((width, hid), BF16),
            pltpu.VMEM((hid, width), BF16),
            pltpu.VMEM((rows, width), BF16),
            pltpu.VMEM((rows, hid), BF16),
            pltpu.VMEM((rows, 2 * hid), BF16),
            pltpu.VMEM((rows, hid), F32),
            pltpu.VMEM((rows, hid), F32),
            pltpu.VMEM((rows, width), F32),
            pltpu.VMEM((half, width), BF16),
            pltpu.VMEM((half, width), BF16),
            pltpu.VMEM((rows, 1), F32),
            pltpu.SemaphoreType.DMA((10 + 2 * len(tiles(width, 512)),)),
        ],
        compiler_params=params(),
        cost_estimate=cost(10 * rows * width * hid, 24e6),
        name="user_layer",
    )(place, hist_len, x, og, hist, item_row, gain, w_gate, w_up, w_down)


def grad_rows(normed_ref, masked_ref, d_both_ref, hidden_ref):
    return (
        mm(normed_ref[...], d_both_ref[...], FIRST),
        mm(masked_ref[...], hidden_ref[...], FIRST),
    )


def sent_kernel(table_ref, normed_ref, masked_ref, d_both_ref, hidden_ref, out_ref):
    cut = d_both_ref.shape[1]
    both, down = grad_rows(normed_ref, masked_ref, d_both_ref, hidden_ref)
    out_ref[0, :, :cut] = both.astype(BF16)
    out_ref[0, :, cut:] = down.astype(BF16)


def kept_kernel(
    place_ref, table_ref, normed_ref, masked_ref, d_both_ref, hidden_ref, got_ref,
    sent_a, kept_a, sent_b, kept_b,
):
    step = pl.program_id(0)
    hid = hidden_ref.shape[1]
    cut = got_ref.shape[1] // 2
    found = grad_rows(normed_ref, masked_ref, d_both_ref, hidden_ref)
    for first, sent, kept, flag in ((0, sent_a, kept_a, 3), (cut, sent_b, kept_b, 6)):
        for piece, at in zip(found, (slice(0, 2 * hid), slice(2 * hid, 3 * hid))):
            value = piece[first : first + cut] + got_ref[0, first : first + cut, at].astype(F32)
            value = value.astype(BF16)

            @pl.when(table_ref[flag, step] == 1)
            def _(sent=sent, value=value, at=at):
                sent[0, :, at] = value

            @pl.when(table_ref[flag, step] == 0)
            def _(kept=kept, value=value, at=at):
                kept[0, :, at] = value


def lhs_specs(rows, block, hid, column_of):
    if block % 128:
        column = pl.BlockSpec((None, rows, block), lambda s, *t: (s, 0, 0))
    else:
        column = pl.BlockSpec((rows, block), lambda s, *t: (0, column_of(s, *t)))
    return [column, column, whole_spec((rows, 2 * hid)), whole_spec((rows, hid))]


def lhs_arrays(columns, normed, masked, block):
    if block % 128 == 0:
        return normed, masked
    return tuple(
        jnp.take(jnp.swapaxes(a.reshape(a.shape[0], -1, block), 0, 1), columns, axis=0)
        for a in (normed, masked)
    )


def sent_grads(place, columns, normed, masked, d_both, hidden, block):
    rows, hid = hidden.shape
    count = columns.shape[0]
    return pl.pallas_call(
        sent_kernel,
        grid_spec=pltpu.PrefetchScalarGridSpec(
            num_scalar_prefetch=1,
            grid=(count,),
            in_specs=lhs_specs(rows, block, hid, lambda s, t: (t[0] ^ s) * 2 + 1 - t[1]),
            out_specs=pl.BlockSpec((1, block, 3 * hid), lambda s, t: (s, 0, 0)),
        ),
        out_shape=jax.ShapeDtypeStruct((count, block, 3 * hid), BF16),
        compiler_params=params(),
        cost_estimate=cost(6 * rows * block * count * hid, 10e6),
        name="sent_grads",
    )(place, *lhs_arrays(columns, normed, masked, block), d_both, hidden)


def kept_grads(place, table, columns, normed, masked, d_both, hidden, got, block):
    rows, hid = hidden.shape
    count = table.shape[1]
    piece = jax.ShapeDtypeStruct((count // 2, block // 2, 3 * hid), BF16)

    def out(row):
        return pl.BlockSpec((1, block // 2, 3 * hid), lambda s, p, t: (t[row, s], 0, 0))

    return pl.pallas_call(
        kept_kernel,
        grid_spec=pltpu.PrefetchScalarGridSpec(
            num_scalar_prefetch=2,
            grid=(count,),
            in_specs=lhs_specs(rows, block, hid, lambda s, p, t: (p[0] ^ t[0, s]) * 2 + p[1])
            + [pl.BlockSpec((1, block, 3 * hid), lambda s, p, t: (t[0, s], 0, 0))],
            out_specs=[out(1), out(2), out(4), out(5)],
        ),
        out_shape=[piece] * 4,
        compiler_params=params(),
        cost_estimate=cost(6 * rows * block * count * hid, 15e6),
        name="kept_grads",
    )(place, jnp.asarray(table), *lhs_arrays(columns, normed, masked, block), d_both, hidden, got)


def forward_kernel(count, n_narrow, place_ref, gain_ref, *refs):
    feats, (gate_hbm, up_hbm) = refs[:count], refs[count : count + 2]
    normed_out, hidden_out, slope_up_out, slope_gate_out = refs[count + 2 : count + 6]
    x, normed, gate, up, gate_act, hidden, slope_up, slope_gate, sems = refs[count + 6 :]
    width, hid = gate.shape
    all_rows = x.shape[0]
    first_sem = count + 3 + 3 * len(tiles(hid, TILE))
    rows = all_rows // count
    share = rows // n_narrow
    pieces = []
    for k in range(count):
        for j in range(n_narrow):
            src = feats[k].at[pl.ds(pl.multiple_of((place_ref[3] ^ j) * share, share), share)]
            to = x.at[pl.ds(k * rows + j * share, share)]
            pieces.append(pltpu.make_async_copy(src, to, sems.at[first_sem + k * n_narrow + j]))
    gate_load = pltpu.make_async_copy(gate_hbm, gate, sems.at[count])
    up_load = pltpu.make_async_copy(up_hbm, up, sems.at[count + 1])
    halves = [range(count // 2), range(count // 2, count)]
    for k in halves[0]:
        for j in range(n_narrow):
            pieces[k * n_narrow + j].start()
    gate_load.start()
    gain = gain_ref[...].reshape(1, width).astype(F32)

    def normalise(k):
        for at in tiles(rows, 64):
            at = slice(k * rows + at.start, k * rows + at.stop)
            part = x[at, :].astype(F32)
            inv = lax.rsqrt(jnp.mean(part * part, axis=1, keepdims=True) + 1e-05)
            normed[at, :] = (part * inv * gain).astype(BF16)

    for k in halves[0]:
        for j in range(n_narrow):
            pieces[k * n_narrow + j].wait()
    for k in halves[1]:
        for j in range(n_narrow):
            pieces[k * n_narrow + j].start()
    up_load.start()
    for k in halves[0]:
        normalise(k)
    gate_load.wait()
    for h in range(2):
        part = slice(h * all_rows // 2, (h + 1) * all_rows // 2)
        if h == 1:
            for k in halves[1]:
                for j in range(n_narrow):
                    pieces[k * n_narrow + j].wait()
            for k in halves[1]:
                normalise(k)
        for at in tiles(hid, TILE):
            gate_act[part, at] = mm(normed[part, :], gate[:, at])
    block = normed_out.shape[1]
    mine = normed
    if block < width:
        mine = normed.at[:, pl.ds(pl.multiple_of(place_ref[2] * block, 128), block)]
    stores = [pltpu.make_async_copy(mine, normed_out, sems.at[count + 2])]
    stores[0].start()
    up_load.wait()
    for at in tiles(hid, TILE):
        up_part = mm(normed[...], up[:, at])
        gate_part = gate_act[:, at]
        sig = 1.0 / (1.0 + jnp.exp(-gate_part))
        silu = gate_part * sig
        hidden[:, at] = (silu * up_part).astype(BF16)
        slope_up[:, at] = silu.astype(BF16)
        slope_gate[:, at] = (up_part * sig * (1.0 + gate_part * (1.0 - sig))).astype(BF16)
        for src, dst in ((hidden, hidden_out), (slope_up, slope_up_out), (slope_gate, slope_gate_out)):
            sem = sems.at[count + 2 + len(stores)]
            stores.append(pltpu.make_async_copy(src.at[:, at], dst.at[:, at], sem))
            stores[-1].start()
    for store in stores:
        store.wait()


def item_forward(place, gain, feats, w_gate, w_up, block, n_narrow):
    count = len(feats)
    rows, width = count * feats[0].shape[0], feats[0].shape[1]
    hid = w_gate.shape[1]
    kept = width if block % 128 else block
    narrow = jax.ShapeDtypeStruct((rows, hid), BF16)
    return pl.pallas_call(
        functools.partial(forward_kernel, count, n_narrow),
        in_specs=[smem(), vmem()] + [hbm()] * (count + 2),
        out_specs=[hbm()] * 4,
        out_shape=[jax.ShapeDtypeStruct((rows, kept), BF16)] + [narrow] * 3,
        scratch_shapes=[
            pltpu.VMEM((rows, width), BF16),
            pltpu.VMEM((rows, width), BF16),
            pltpu.VMEM((width, hid), BF16),
            pltpu.VMEM((width, hid), BF16),
            pltpu.VMEM((rows, hid), F32),
            pltpu.VMEM((rows, hid), BF16),
            pltpu.VMEM((rows, hid), BF16),
            pltpu.VMEM((rows, hid), BF16),
            pltpu.SemaphoreType.DMA((count + 3 + 3 * len(tiles(hid, TILE)) + count * n_narrow,)),
        ],
        compiler_params=params(),
        cost_estimate=cost(4 * rows * width * hid, 16e6),
        name="item_forward",
    )(place, gain, *feats, w_gate, w_up)


def own_kernel(cot, slope_up, slope_gate, gate_hbm, up_hbm, down_hbm, *refs):
    outs, (total, gate, up, down, sems) = refs[:-5], refs[-5:]
    loads = [
        pltpu.make_async_copy(src, dst, sems.at[k])
        for k, (src, dst) in enumerate(((down_hbm, down), (gate_hbm, gate), (up_hbm, up)))
    ]
    for load in loads:
        load.start()
    loads[0].wait()
    d_hidden = mm(cot[...], down[...], LAST)
    d_up = (d_hidden * slope_up[...].astype(F32)).astype(BF16)
    d_gate = (d_hidden * slope_gate[...].astype(F32)).astype(BF16)
    loads[1].wait()
    loads[2].wait()
    for at in tiles(total.shape[1], 512):
        total[:, at] = (mm(d_gate, gate[at, :], LAST) + mm(d_up, up[at, :], LAST)).astype(BF16)
    share = outs[0].shape[0]
    for k, out in enumerate(outs):
        out[...] = total[k * share : (k + 1) * share, :]


def item_own(cot, slope_up, slope_gate, w_gate, w_up, w_down, n_narrow):
    rows, width = cot.shape
    hid = w_gate.shape[1]
    part = (rows // n_narrow, width)
    return pl.pallas_call(
        own_kernel,
        grid=(1,),
        in_specs=[whole_spec((rows, width)), whole_spec((rows, hid)), whole_spec((rows, hid))]
        + [hbm()] * 3,
        out_specs=[whole_spec(part)] * n_narrow,
        out_shape=[jax.ShapeDtypeStruct(part, BF16)] * n_narrow,
        scratch_shapes=[
            pltpu.VMEM((rows, width), BF16),
            pltpu.VMEM((width, hid), BF16),
            pltpu.VMEM((width, hid), BF16),
            pltpu.VMEM((hid, width), BF16),
            pltpu.SemaphoreType.DMA((3,)),
        ],
        compiler_params=params(),
        cost_estimate=cost(6 * rows * width * hid, 11e6),
        name="item_own",
    )(cot, slope_up, slope_gate, w_gate, w_up, w_down)


def late_kernel(slots, before, scale, place_ref, *refs):
    count = len(slots)
    pieces, (column_hbm, normed_hbm, hidden_hbm, slope_up_hbm, slope_gate_hbm, down_hbm) = (
        refs[:count],
        refs[count : count + 6],
    )
    earlier, refs = (refs[count + 6 : count + 9], refs[count + 9 :]) if before else (None, refs[count + 6 :])
    outs, (cot, column, normed, hidden, slope_up, slope_gate, d_both, down, sems) = refs[:3], refs[3:]
    rows = cot.shape[0] // count
    block = column.shape[1]
    narrow = block % 128 != 0
    hid = hidden.shape[1]
    copies = [(piece, cot.at[pl.ds(k * rows, rows)]) for k, piece in enumerate(pieces)]
    copies += [(down_hbm.at[to], down.at[to]) for to in tiles(hid, TILE)]
    for k, slot in enumerate(slots):
        at, to = pl.ds(slot * rows, rows), pl.ds(k * rows, rows)
        copies += [(slope_up_hbm.at[at], slope_up.at[to]), (slope_gate_hbm.at[at], slope_gate.at[to])]
        copies += [(normed_hbm.at[at], normed.at[to]), (hidden_hbm.at[at], hidden.at[to])]
    if narrow:
        copies.append((column_hbm, column))
    loads = [pltpu.make_async_copy(src, dst, sems.at[k]) for k, (src, dst) in enumerate(copies)]
    for load in loads:
        load.start()
    for load in loads[:count]:
        load.wait()
    if not narrow:
        column[...] = cot[:, pl.ds(pl.multiple_of(place_ref[2] * block, 128), block)]
    downs, rest = loads[count : count + len(tiles(hid, TILE))], loads[count + len(tiles(hid, TILE)) :]
    for k, to in enumerate(tiles(hid, TILE)):
        downs[k].wait()
        d_hidden = mm(cot[...], down[to, :], LAST)
        if k == 0:
            for load in rest:
                load.wait()
        d_both[:, to] = (d_hidden * slope_gate[:, to].astype(F32)).astype(BF16)
        at = slice(hid + to.start, hid + to.stop)
        d_both[:, at] = (d_hidden * slope_up[:, to].astype(F32)).astype(BF16)
    both_part = mm(normed[...], d_both[...], FIRST) * scale
    down_part = mm(column[...], hidden[...], FIRST).T * scale
    parts = (both_part[:, :hid], both_part[:, hid:], down_part)
    for k, part in enumerate(parts):
        outs[k][...] = part + earlier[k][...] if before else part


def item_late(place, slots, pieces, column, normed, hidden, slope_up, slope_gate, w_down, before, scale):
    count = len(pieces)
    rows, width = count * pieces[0].shape[0], pieces[0].shape[1]
    hid, block = w_down.shape[0], normed.shape[1]
    before = list(before) if before is not None else []
    return pl.pallas_call(
        functools.partial(late_kernel, tuple(slots), bool(before), scale),
        in_specs=[smem()] + [hbm()] * (count + 6) + [vmem()] * len(before),
        out_specs=[vmem()] * 3,
        out_shape=[
            jax.ShapeDtypeStruct((block, hid), F32),
            jax.ShapeDtypeStruct((block, hid), F32),
            jax.ShapeDtypeStruct((hid, block), F32),
        ],
        scratch_shapes=[
            pltpu.VMEM((rows, width), BF16),
            pltpu.VMEM((rows, block), BF16),
            pltpu.VMEM((rows, block), BF16),
            pltpu.VMEM((rows, hid), BF16),
            pltpu.VMEM((rows, hid), BF16),
            pltpu.VMEM((rows, hid), BF16),
            pltpu.VMEM((rows, 2 * hid), BF16),
            pltpu.VMEM((hid, width), BF16),
            pltpu.SemaphoreType.DMA((5 * count + 1 + len(tiles(hid, TILE)),)),
        ],
        compiler_params=params(),
        cost_estimate=cost(4 * rows * width * hid + 12 * rows * block * hid, 16e6),
        name="item_late",
    )(
        place, *pieces, column, normed, hidden, slope_up, slope_gate, w_down, *before,
    )


def merge_kernel(here_ref, kept_ref, got_ref, *refs):
    count = sum(1 for r in refs if r.shape == kept_ref.shape) - 1
    pieces, outs, total = refs[:count], refs[count:-1], refs[-1]
    value = kept_ref[...].astype(F32) + got_ref[...].astype(F32)
    for piece in pieces:
        value = value + piece[...].astype(F32)
    total[...] = value.astype(BF16)
    cut_rows(here_ref[0], total, outs)


def cut_rows(here, total, outs):
    rows = outs[0].shape[0]
    for k, out in enumerate(outs):
        out[...] = total[pl.ds(pl.multiple_of((here ^ k) * rows, rows), rows), :]


def merge_chips(here, kept, got, pieces, n_narrow):
    rows, width = pieces[0].shape
    spec = whole_spec((rows, width))
    part = (rows // n_narrow, width)
    return pl.pallas_call(
        merge_kernel,
        grid=(1,),
        in_specs=[smem()] + [spec] * (2 + len(pieces)),
        out_specs=[whole_spec(part)] * n_narrow,
        out_shape=[jax.ShapeDtypeStruct(part, BF16)] * n_narrow,
        scratch_shapes=[pltpu.VMEM((rows, width), BF16)],
        compiler_params=params(),
        cost_estimate=cost(0, 2 * (4 + len(pieces)) * rows * width),
        name="merge_chips",
    )(jnp.reshape(here, (1,)), kept, got, *pieces)


def final_kernel(scale, here_ref, kept_a, got_a, kept_b, got_b, *refs):
    slots, (feat_out, gate_out, up_out, down_out) = refs[:-4], refs[-4:]
    cut, hid = kept_a.shape[0], gate_out.shape[1]
    for half, (kept, got) in enumerate(((kept_a, got_a), (kept_b, got_b))):
        total = (kept[...].astype(F32) + got[...].astype(F32)) * scale
        at = slice(half * cut, (half + 1) * cut)
        gate_out[at, :] = total[:, :hid]
        up_out[at, :] = total[:, hid : 2 * hid]
        down_out[:, at] = total[:, 2 * hid :].T
    rows = slots[0].shape[0]
    for k, slot in enumerate(slots):
        feat_out[pl.ds(pl.multiple_of((here_ref[0] ^ k) * rows, rows), rows), :] = slot[...]


def final_sums(here, kept_a, got_a, kept_b, got_b, slots, scale):
    cut, hid = kept_a.shape[0], kept_a.shape[1] // 3
    rows, width = slots[0].shape
    return pl.pallas_call(
        functools.partial(final_kernel, scale),
        in_specs=[smem()] + [vmem()] * (4 + len(slots)),
        out_specs=[vmem()] * 4,
        out_shape=[
            jax.ShapeDtypeStruct((len(slots) * rows, width), BF16),
            jax.ShapeDtypeStruct((2 * cut, hid), F32),
            jax.ShapeDtypeStruct((2 * cut, hid), F32),
            jax.ShapeDtypeStruct((hid, 2 * cut), F32),
        ],
        compiler_params=params(),
        cost_estimate=cost(0, 30 * cut * hid),
        name="final_sums",
    )(jnp.reshape(here, (1,)), kept_a, got_a, kept_b, got_b, *slots)


def grad_tables(n_chips, order_a, order_b):
    first_a, first_b = order_a[0] >> 1, order_b[0] >> 1
    rels = sorted(range(n_chips), key=lambda r: (not (r & first_a), not (r & first_b), r))
    rows = [[], [], [], [], [], [], []]
    places = {}
    for name, first, row in (("a", first_a, 0), ("b", first_b, 3)):
        sent_order = [r for r in rels if r & first]
        kept_order = [r for r in rels if not r & first]
        last_sent = last_kept = 0
        for r in rels:
            is_sent = bool(r & first)
            if is_sent:
                last_sent = sent_order.index(r)
            else:
                last_kept = kept_order.index(r)
            rows[row].append(last_sent)
            rows[row + 1].append(last_kept)
            rows[row + 2].append(int(is_sent))
        places[name] = kept_order
    return np.array([rels, *rows[:6]], np.int32), places


def first_sums(got, kept, slots):
    return {r: (kept[i].astype(F32) + got[i].astype(F32)).astype(BF16) for i, r in enumerate(slots)}


def sent_away(total, bit):
    away = sorted(r for r in total if r & (bit >> 1))
    return jnp.stack([total[r] for r in away])


def next_sums(total, got, bit):
    away = sorted(r for r in total if r & (bit >> 1))
    return {
        r ^ (bit >> 1): (total[r ^ (bit >> 1)].astype(F32) + got[i].astype(F32)).astype(BF16)
        for i, r in enumerate(away)
    }


def body(
    user_input,
    out_grad,
    hist_len,
    hist_items,
    item_row,
    item_feat,
    user_gain,
    user_gate,
    user_up,
    user_down,
    item_gain,
    item_gate,
    item_up,
    item_down,
):
    n_wide, n_narrow = lax.axis_size("wide"), lax.axis_size("narrow")
    me, here = lax.axis_index("wide"), lax.axis_index("narrow")
    chip, core = me // 2, me % 2
    n_chips = n_wide // 2
    bits = [1 << k for k in range(1, n_wide.bit_length() - 1)]
    order_a = bits
    order_b = bits[len(bits) // 2 :] + bits[: len(bits) // 2]
    user_count, hist_length, width = user_input.shape
    rows = user_count * hist_length
    item_dev = item_feat.shape[0]
    hid = user_gate.shape[1]
    block = width // n_wide
    rels = jnp.arange(n_chips, dtype=jnp.int32)
    place = jnp.stack([chip, core, me, here])

    def near(value):
        return [value] + [swap(value, r << 1) for r in range(1, n_chips)]

    def gather_wide(value):
        pieces = near(value)
        return pieces + [swap(piece, 1) for piece in pieces]

    feats = gather_wide(item_feat)

    normed, masked, hidden, d_both, sent, kept = user_layer(
        place,
        hist_len,
        user_input.reshape(rows, width),
        out_grad.reshape(rows, width),
        hist_items,
        item_row,
        user_gain,
        user_gate,
        user_up,
        user_down,
        1.0 / n_narrow,
        item_dev,
    )
    sent, *_ = lax.optimization_barrier((sent, *feats[1:n_chips]))
    got = swap(sent, 1)
    grads_sent = sent_grads(place, (chip ^ rels) * 2 + 1 - core, normed, masked, d_both, hidden, block)
    got, grads_sent = lax.optimization_barrier((got, grads_sent))
    grads_got = swap(grads_sent, 1)
    sums = []
    for r in range(1, n_chips):
        at = slice(r * item_dev, (r + 1) * item_dev)
        sums.append((kept[at].astype(F32) + got[at].astype(F32)).astype(BF16))
    pieces = [swap(total, r << 1) for r, total in enumerate(sums, 1)]

    group = min(8, n_wide)
    forwards = [
        item_forward(place, item_gain, feats[k : k + group], item_gate, item_up, block, n_narrow)
        for k in range(0, n_wide, group)
    ]

    kept_table, places = grad_tables(n_chips, order_a, order_b)
    grads_got, _ = lax.optimization_barrier((grads_got, forwards[-1][0]))
    sent_a, kept_a, sent_b, kept_b = kept_grads(
        place, kept_table, (chip ^ jnp.asarray(kept_table[0])) * 2 + core,
        normed, masked, d_both, hidden, grads_got, block,
    )
    pieces[0], sent_a, sent_b = lax.optimization_barrier((pieces[0], sent_a, sent_b))
    mine = list(merge_chips(here, kept, got, pieces, n_narrow))
    sent_a, sent_b, mine[0] = lax.optimization_barrier((sent_a, sent_b, mine[0]))
    got_a, got_b = swap(sent_a, order_a[0]), swap(sent_b, order_b[0])

    quarter = item_dev // n_narrow

    def narrow_scatter(parts):
        got = [
            part if k == 0 else lax.ppermute(part, "narrow", [(i, i ^ k) for i in range(n_narrow)])
            for k, part in enumerate(parts)
        ]
        return functools.reduce(jnp.add, [part.astype(F32) for part in got])

    def narrow_slots(piece):
        return [piece] + [
            lax.ppermute(piece, "narrow", [(i, i ^ k) for i in range(n_narrow)])
            for k in range(1, n_narrow)
        ]

    item_in = narrow_scatter(mine)
    item_cot = jnp.concatenate(narrow_slots(item_in.astype(BF16)), axis=0)
    cots = [item_cot] + [swap(item_cot, r << 1) for r in range(1, n_chips - 1)]
    last_cot, *cots[1:] = lax.optimization_barrier((item_cot, *cots[1:]))
    cots.append(swap(last_cot, (n_chips - 1) << 1))
    item_part = item_own(
        item_cot, forwards[0][2], forwards[0][3], item_gate, item_up, item_down, n_narrow
    )
    item_dn = narrow_scatter(item_part)

    got_a, got_b, _ = lax.optimization_barrier((got_a, got_b, item_part[0]))
    assert len(order_a) > 1
    total_a = first_sums(got_a, kept_a, places["a"])
    total_b = first_sums(got_b, kept_b, places["b"])
    for a, b in zip(order_a[1:], order_b[1:]):
        away_a, away_b = sent_away(total_a, a), sent_away(total_b, b)
        away_a, away_b, cots[1] = lax.optimization_barrier((away_a, away_b, cots[1]))
        got_a, got_b = swap(away_a, a), swap(away_b, b)
        if a != order_a[-1]:
            total_a, total_b = next_sums(total_a, got_a, a), next_sums(total_b, got_b, b)
    cots = cots + [swap(piece, 1) for piece in cots]

    slots = range(n_wide)
    if n_wide == group:
        arrived = [k for k in slots if k % n_chips != n_chips - 1]
        lots = [arrived, [k for k in slots if k not in arrived]]
    else:
        lots = [list(slots[k : k + group]) for k in range(0, n_wide, group)]

    def late(lot, before):
        normed_k, hidden_k, slope_up_k, slope_gate_k = forwards[lot[0] // group]
        parts = [cots[k] for k in lot]
        column = parts[0]
        if block % 128:
            normed_k = lax.dynamic_slice_in_dim(normed_k, me * block, block, axis=1)
            column = jnp.concatenate(
                [lax.dynamic_slice_in_dim(p, me * block, block, axis=1) for p in parts], axis=0
            )
        return list(
            item_late(
                place, [k % group for k in lot], parts, column, normed_k, hidden_k, slope_up_k,
                slope_gate_k, item_down, before, 1.0 / n_wide,
            )
        )

    item_grads = late(lots[0], None)
    own_feat = lax.dynamic_slice_in_dim(item_feat, here * quarter, quarter, axis=0)
    own_feat, item_in, item_grads[0] = lax.optimization_barrier((own_feat, item_in, item_grads[0]))
    item_scaled = item_gain.astype(F32)[None, :] * item_dn
    own = own_feat.astype(F32)
    own_inv = lax.rsqrt(jnp.mean(own * own, axis=1, keepdims=True) + 1e-05)
    own_unit = own * own_inv
    item_mean = jnp.mean(item_scaled * own_unit, axis=1, keepdims=True)
    feat_rows = (item_in + own_inv * (item_scaled - own_unit * item_mean)).astype(BF16)
    feat_slots = narrow_slots(feat_rows)

    for lot in lots[1:]:
        item_grads = late(lot, item_grads)

    got_a, got_b, item_grads[0], *feat_slots = lax.optimization_barrier(
        (got_a, got_b, item_grads[0], *feat_slots)
    )
    feat_grad, *user_grads = final_sums(
        here, total_a[0], got_a[0], total_b[0], got_b[0], feat_slots, 1.0 / n_wide
    )
    return (feat_grad, *user_grads, *item_grads)


def solution(mesh):
    placed = (
        P("wide", None, None),
        P("wide", None, None),
        P("wide"),
        P("wide", None),
        P(),
        P("wide", None),
        P(),
        P(None, "narrow"),
        P(None, "narrow"),
        P("narrow", None),
        P(),
        P(None, "narrow"),
        P(None, "narrow"),
        P("narrow", None),
    )
    return jax.shard_map(
        body,
        mesh=mesh,
        in_specs=placed,
        out_specs=(
            P("wide", None),
            P("wide", "narrow"),
            P("wide", "narrow"),
            P("narrow", "wide"),
            P("wide", "narrow"),
            P("wide", "narrow"),
            P("narrow", "wide"),
        ),
        check_vma=False,
    )
```

```python
import functools

import jax
import jax.numpy as jnp
import numpy as np
from jax import lax
from jax.experimental import pallas as pl
from jax.experimental.pallas import tpu as pltpu
from jax.sharding import PartitionSpec as P

F32 = jnp.float32
BF16 = jnp.bfloat16
LAST = (((1,), (1,)), ((), ()))
FIRST = (((0,), (0,)), ((), ()))
PLAIN = (((1,), (0,)), ((), ()))
TILE = 256


def mm(a, b, dims=PLAIN):
    return lax.dot_general(a, b, dims, preferred_element_type=F32)


def params():
    return pltpu.CompilerParams(vmem_limit_bytes=60 << 20)


def cost(flops, touched):
    return pl.CostEstimate(flops=int(flops) // 6, bytes_accessed=int(touched) // 6, transcendentals=0)


def hbm():
    return pl.BlockSpec(memory_space=pl.ANY)


def vmem():
    return pl.BlockSpec(memory_space=pltpu.VMEM)


def smem():
    return pl.BlockSpec(memory_space=pltpu.SMEM)


def whole_spec(shape):
    return pl.BlockSpec(shape, lambda *_: (0,) * len(shape))


def swap(value, bit):
    count = lax.axis_size("wide")
    return lax.ppermute(value, "wide", [(i, i ^ bit) for i in range(count)])


def after(value, *others):
    return lax.optimization_barrier((value, *others))[0]


def tiles(total, size):
    size = min(size, total)
    return [slice(k, k + size) for k in range(0, total, size)]


def segment_picks(place, parity, targets, item_dev, count):
    column = lax.broadcasted_iota(jnp.int32, (1, count), 1)
    block = (place ^ (column // item_dev)) * 2 + parity
    return (targets == block * item_dev + column % item_dev).astype(BF16)


def user_kernel(
    share, item_dev, place_ref, hist_len_ref, x_hbm, og_hbm, hist_ref, item_row_ref, gain_ref,
    gate_hbm, up_hbm, down_hbm,
    normed_out, masked_out, hidden_out, d_both_out, sent_out, kept_out,
    x, og, gate, up, down, normed, hidden, d_both, gate_act, up_act, total, sent, kept, inv_ref,
    sems,
):
    loads = [
        pltpu.make_async_copy(src, dst, sems.at[k])
        for k, (src, dst) in enumerate(
            ((x_hbm, x), (gate_hbm, gate), (up_hbm, up), (og_hbm, og), (down_hbm, down))
        )
    ]
    for load in loads[:2]:
        load.start()
    stores = [
        pltpu.make_async_copy(src, dst, sems.at[5 + k])
        for k, (src, dst) in enumerate(
            (
                (normed, normed_out),
                (og, masked_out),
                (hidden, hidden_out),
                (d_both, d_both_out),
            )
        )
    ]
    rows, width = x.shape
    users, length = hist_ref.shape
    hid = hidden.shape[1]
    gain = gain_ref[...].reshape(1, width).astype(F32)

    square = (length, length)
    diagonal = lax.broadcasted_iota(jnp.int32, square, 0) == lax.broadcasted_iota(jnp.int32, square, 1)
    item_row = item_row_ref[...].reshape(1, -1)
    ids = lax.broadcasted_iota(jnp.int32, (1, item_row.shape[1]), 1)
    targets = []
    for u in range(users):
        items = jnp.sum(jnp.where(diagonal, hist_ref[u : u + 1, :], 0), axis=1, keepdims=True)
        targets.append(jnp.sum(jnp.where(items == ids, item_row, 0), axis=1, keepdims=True))
    targets = jnp.concatenate(targets, axis=0)

    loads[0].wait()
    for load in loads[2:]:
        load.start()
    for at in tiles(rows, 64):
        part = x[at, :].astype(F32)
        inv = lax.rsqrt(jnp.mean(part * part, axis=1, keepdims=True) + 1e-05)
        inv_ref[at, :] = inv
        normed[at, :] = (part * inv * gain).astype(BF16)
    stores[0].start()
    loads[1].wait()
    for at in tiles(hid, TILE):
        gate_act[:, at] = mm(normed[...], gate[:, at])
    loads[2].wait()
    for at in tiles(hid, TILE):
        up_act[:, at] = mm(normed[...], up[:, at])
    loads[3].wait()
    place = lax.broadcasted_iota(jnp.int32, (length, 1), 0)
    for u in range(users):
        at = slice(u * length, (u + 1) * length)
        og[at, :] = jnp.where(place < hist_len_ref[u], og[at, :].astype(F32), 0.0).astype(BF16)
    stores[1].start()
    loads[4].wait()
    for at in tiles(hid, TILE):
        d_hidden = mm(og[...], down[at, :], LAST)
        gate_part, up_part = gate_act[:, at], up_act[:, at]
        sig = 1.0 / (1.0 + jnp.exp(-gate_part))
        silu = gate_part * sig
        hidden[:, at] = (silu * up_part).astype(BF16)
        d_both[:, hid + at.start : hid + at.stop] = (d_hidden * silu).astype(BF16)
        d_both[:, at] = (d_hidden * up_part * sig * (1.0 + gate_part * (1.0 - sig))).astype(BF16)
    for k in (2, 3):
        stores[k].start()
    mean = jnp.zeros((rows, 1), F32)
    inv = inv_ref[...]
    for at in tiles(width, 512):
        part = mm(d_both[:, :hid], gate[at, :], LAST) + mm(d_both[:, hid:], up[at, :], LAST)
        part = part * gain[:, at]
        total[:, at] = part
        mean = mean + jnp.sum(part * (x[:, at].astype(F32) * inv), axis=1, keepdims=True)
    slope = inv * inv * mean * (1.0 / width)
    chip, core = place_ref[0], place_ref[1]
    half = sent.shape[0]
    picks_sent = segment_picks(chip, 1 - core, targets, item_dev, half)
    picks_kept = segment_picks(chip, core, targets, item_dev, half)
    for at in tiles(width, 512):
        occ = (
            og[:, at].astype(F32) * share + inv * total[:, at] - x[:, at].astype(F32) * slope
        ).astype(BF16)
        sent[:, at] = mm(picks_sent, occ, FIRST).astype(BF16)
        kept[:, at] = mm(picks_kept, occ, FIRST).astype(BF16)
        for src, dst in ((sent, sent_out), (kept, kept_out)):
            stores.append(pltpu.make_async_copy(src.at[:, at], dst.at[:, at], sems.at[5 + len(stores)]))
            stores[-1].start()
    for store in stores:
        store.wait()


def user_layer(place, hist_len, x, og, hist, item_row, gain, w_gate, w_up, w_down, share, item_dev):
    rows, width = x.shape
    hid = w_gate.shape[1]
    half = item_row.shape[0] // 2
    wide = jax.ShapeDtypeStruct((rows, width), BF16)
    narrow = jax.ShapeDtypeStruct((rows, hid), BF16)
    summed = jax.ShapeDtypeStruct((half, width), BF16)
    return pl.pallas_call(
        functools.partial(user_kernel, share, item_dev),
        in_specs=[smem()] * 2 + [hbm()] * 2 + [vmem()] * 3 + [hbm()] * 3,
        out_specs=[hbm()] * 6,
        out_shape=[wide, wide, narrow, jax.ShapeDtypeStruct((rows, 2 * hid), BF16), summed, summed],
        scratch_shapes=[
            pltpu.VMEM((rows, width), BF16),
            pltpu.VMEM((rows, width), BF16),
            pltpu.VMEM((width, hid), BF16),
            pltpu.VMEM((width, hid), BF16),
            pltpu.VMEM((hid, width), BF16),
            pltpu.VMEM((rows, width), BF16),
            pltpu.VMEM((rows, hid), BF16),
            pltpu.VMEM((rows, 2 * hid), BF16),
            pltpu.VMEM((rows, hid), F32),
            pltpu.VMEM((rows, hid), F32),
            pltpu.VMEM((rows, width), F32),
            pltpu.VMEM((half, width), BF16),
            pltpu.VMEM((half, width), BF16),
            pltpu.VMEM((rows, 1), F32),
            pltpu.SemaphoreType.DMA((10 + 2 * len(tiles(width, 512)),)),
        ],
        compiler_params=params(),
        cost_estimate=cost(10 * rows * width * hid, 24e6),
        name="user_layer",
    )(place, hist_len, x, og, hist, item_row, gain, w_gate, w_up, w_down)


def grad_rows(normed_ref, masked_ref, d_both_ref, hidden_ref):
    return (
        mm(normed_ref[...], d_both_ref[...], FIRST),
        mm(masked_ref[...], hidden_ref[...], FIRST),
    )


def sent_kernel(table_ref, normed_ref, masked_ref, d_both_ref, hidden_ref, out_ref):
    cut = d_both_ref.shape[1]
    both, down = grad_rows(normed_ref, masked_ref, d_both_ref, hidden_ref)
    out_ref[0, :, :cut] = both.astype(BF16)
    out_ref[0, :, cut:] = down.astype(BF16)


def kept_kernel(
    place_ref, table_ref, normed_ref, masked_ref, d_both_ref, hidden_ref, got_ref,
    sent_a, kept_a, sent_b, kept_b,
):
    step = pl.program_id(0)
    hid = hidden_ref.shape[1]
    cut = got_ref.shape[1] // 2
    found = grad_rows(normed_ref, masked_ref, d_both_ref, hidden_ref)
    for first, sent, kept, flag in ((0, sent_a, kept_a, 3), (cut, sent_b, kept_b, 6)):
        for piece, at in zip(found, (slice(0, 2 * hid), slice(2 * hid, 3 * hid))):
            value = piece[first : first + cut] + got_ref[0, first : first + cut, at].astype(F32)
            value = value.astype(BF16)

            @pl.when(table_ref[flag, step] == 1)
            def _(sent=sent, value=value, at=at):
                sent[0, :, at] = value

            @pl.when(table_ref[flag, step] == 0)
            def _(kept=kept, value=value, at=at):
                kept[0, :, at] = value


def lhs_specs(rows, block, hid, column_of):
    if block % 128:
        column = pl.BlockSpec((None, rows, block), lambda s, *t: (s, 0, 0))
    else:
        column = pl.BlockSpec((rows, block), lambda s, *t: (0, column_of(s, *t)))
    return [column, column, whole_spec((rows, 2 * hid)), whole_spec((rows, hid))]


def lhs_arrays(columns, normed, masked, block):
    if block % 128 == 0:
        return normed, masked
    return tuple(
        jnp.take(jnp.swapaxes(a.reshape(a.shape[0], -1, block), 0, 1), columns, axis=0)
        for a in (normed, masked)
    )


def sent_grads(place, columns, normed, masked, d_both, hidden, block):
    rows, hid = hidden.shape
    count = columns.shape[0]
    return pl.pallas_call(
        sent_kernel,
        grid_spec=pltpu.PrefetchScalarGridSpec(
            num_scalar_prefetch=1,
            grid=(count,),
            in_specs=lhs_specs(rows, block, hid, lambda s, t: (t[0] ^ s) * 2 + 1 - t[1]),
            out_specs=pl.BlockSpec((1, block, 3 * hid), lambda s, t: (s, 0, 0)),
        ),
        out_shape=jax.ShapeDtypeStruct((count, block, 3 * hid), BF16),
        compiler_params=params(),
        cost_estimate=cost(6 * rows * block * count * hid, 10e6),
        name="sent_grads",
    )(place, *lhs_arrays(columns, normed, masked, block), d_both, hidden)


def kept_grads(place, table, columns, normed, masked, d_both, hidden, got, block):
    rows, hid = hidden.shape
    count = table.shape[1]
    piece = jax.ShapeDtypeStruct((count // 2, block // 2, 3 * hid), BF16)

    def out(row):
        return pl.BlockSpec((1, block // 2, 3 * hid), lambda s, p, t: (t[row, s], 0, 0))

    return pl.pallas_call(
        kept_kernel,
        grid_spec=pltpu.PrefetchScalarGridSpec(
            num_scalar_prefetch=2,
            grid=(count,),
            in_specs=lhs_specs(rows, block, hid, lambda s, p, t: (p[0] ^ t[0, s]) * 2 + p[1])
            + [pl.BlockSpec((1, block, 3 * hid), lambda s, p, t: (t[0, s], 0, 0))],
            out_specs=[out(1), out(2), out(4), out(5)],
        ),
        out_shape=[piece] * 4,
        compiler_params=params(),
        cost_estimate=cost(6 * rows * block * count * hid, 15e6),
        name="kept_grads",
    )(place, jnp.asarray(table), *lhs_arrays(columns, normed, masked, block), d_both, hidden, got)


def forward_kernel(count, n_narrow, place_ref, gain_ref, *refs):
    feats, (gate_hbm, up_hbm) = refs[:count], refs[count : count + 2]
    normed_out, hidden_out, slope_up_out, slope_gate_out = refs[count + 2 : count + 6]
    x, normed, gate, up, gate_act, hidden, slope_up, slope_gate, sems = refs[count + 6 :]
    width, hid = gate.shape
    all_rows = x.shape[0]
    first_sem = count + 3 + 3 * len(tiles(hid, TILE))
    rows = all_rows // count
    share = rows // n_narrow
    pieces = []
    for k in range(count):
        for j in range(n_narrow):
            src = feats[k].at[pl.ds(pl.multiple_of((place_ref[3] ^ j) * share, share), share)]
            to = x.at[pl.ds(k * rows + j * share, share)]
            pieces.append(pltpu.make_async_copy(src, to, sems.at[first_sem + k * n_narrow + j]))
    gate_load = pltpu.make_async_copy(gate_hbm, gate, sems.at[count])
    up_load = pltpu.make_async_copy(up_hbm, up, sems.at[count + 1])
    halves = [range(count // 2), range(count // 2, count)]
    for k in halves[0]:
        for j in range(n_narrow):
            pieces[k * n_narrow + j].start()
    gate_load.start()
    gain = gain_ref[...].reshape(1, width).astype(F32)

    def normalise(k):
        for at in tiles(rows, 64):
            at = slice(k * rows + at.start, k * rows + at.stop)
            part = x[at, :].astype(F32)
            inv = lax.rsqrt(jnp.mean(part * part, axis=1, keepdims=True) + 1e-05)
            normed[at, :] = (part * inv * gain).astype(BF16)

    for k in halves[0]:
        for j in range(n_narrow):
            pieces[k * n_narrow + j].wait()
    for k in halves[1]:
        for j in range(n_narrow):
            pieces[k * n_narrow + j].start()
    up_load.start()
    for k in halves[0]:
        normalise(k)
    gate_load.wait()
    for h in range(2):
        part = slice(h * all_rows // 2, (h + 1) * all_rows // 2)
        if h == 1:
            for k in halves[1]:
                for j in range(n_narrow):
                    pieces[k * n_narrow + j].wait()
            for k in halves[1]:
                normalise(k)
        for at in tiles(hid, TILE):
            gate_act[part, at] = mm(normed[part, :], gate[:, at])
    block = normed_out.shape[1]
    mine = normed
    if block < width:
        mine = normed.at[:, pl.ds(pl.multiple_of(place_ref[2] * block, 128), block)]
    stores = [pltpu.make_async_copy(mine, normed_out, sems.at[count + 2])]
    stores[0].start()
    up_load.wait()
    for at in tiles(hid, TILE):
        up_part = mm(normed[...], up[:, at])
        gate_part = gate_act[:, at]
        sig = 1.0 / (1.0 + jnp.exp(-gate_part))
        silu = gate_part * sig
        hidden[:, at] = (silu * up_part).astype(BF16)
        slope_up[:, at] = silu.astype(BF16)
        slope_gate[:, at] = (up_part * sig * (1.0 + gate_part * (1.0 - sig))).astype(BF16)
        for src, dst in ((hidden, hidden_out), (slope_up, slope_up_out), (slope_gate, slope_gate_out)):
            sem = sems.at[count + 2 + len(stores)]
            stores.append(pltpu.make_async_copy(src.at[:, at], dst.at[:, at], sem))
            stores[-1].start()
    for store in stores:
        store.wait()


def item_forward(place, gain, feats, w_gate, w_up, block, n_narrow):
    count = len(feats)
    rows, width = count * feats[0].shape[0], feats[0].shape[1]
    hid = w_gate.shape[1]
    kept = width if block % 128 else block
    narrow = jax.ShapeDtypeStruct((rows, hid), BF16)
    return pl.pallas_call(
        functools.partial(forward_kernel, count, n_narrow),
        in_specs=[smem(), vmem()] + [hbm()] * (count + 2),
        out_specs=[hbm()] * 4,
        out_shape=[jax.ShapeDtypeStruct((rows, kept), BF16)] + [narrow] * 3,
        scratch_shapes=[
            pltpu.VMEM((rows, width), BF16),
            pltpu.VMEM((rows, width), BF16),
            pltpu.VMEM((width, hid), BF16),
            pltpu.VMEM((width, hid), BF16),
            pltpu.VMEM((rows, hid), F32),
            pltpu.VMEM((rows, hid), BF16),
            pltpu.VMEM((rows, hid), BF16),
            pltpu.VMEM((rows, hid), BF16),
            pltpu.SemaphoreType.DMA((count + 3 + 3 * len(tiles(hid, TILE)) + count * n_narrow,)),
        ],
        compiler_params=params(),
        cost_estimate=cost(4 * rows * width * hid, 16e6),
        name="item_forward",
    )(place, gain, *feats, w_gate, w_up)


def own_kernel(cot, slope_up, slope_gate, gate_hbm, up_hbm, down_hbm, *refs):
    outs, (total, gate, up, down, sems) = refs[:-5], refs[-5:]
    loads = [
        pltpu.make_async_copy(src, dst, sems.at[k])
        for k, (src, dst) in enumerate(((down_hbm, down), (gate_hbm, gate), (up_hbm, up)))
    ]
    for load in loads:
        load.start()
    loads[0].wait()
    d_hidden = mm(cot[...], down[...], LAST)
    d_up = (d_hidden * slope_up[...].astype(F32)).astype(BF16)
    d_gate = (d_hidden * slope_gate[...].astype(F32)).astype(BF16)
    loads[1].wait()
    loads[2].wait()
    for at in tiles(total.shape[1], 512):
        total[:, at] = (mm(d_gate, gate[at, :], LAST) + mm(d_up, up[at, :], LAST)).astype(BF16)
    share = outs[0].shape[0]
    for k, out in enumerate(outs):
        out[...] = total[k * share : (k + 1) * share, :]


def item_own(cot, slope_up, slope_gate, w_gate, w_up, w_down, n_narrow):
    rows, width = cot.shape
    hid = w_gate.shape[1]
    part = (rows // n_narrow, width)
    return pl.pallas_call(
        own_kernel,
        grid=(1,),
        in_specs=[whole_spec((rows, width)), whole_spec((rows, hid)), whole_spec((rows, hid))]
        + [hbm()] * 3,
        out_specs=[whole_spec(part)] * n_narrow,
        out_shape=[jax.ShapeDtypeStruct(part, BF16)] * n_narrow,
        scratch_shapes=[
            pltpu.VMEM((rows, width), BF16),
            pltpu.VMEM((width, hid), BF16),
            pltpu.VMEM((width, hid), BF16),
            pltpu.VMEM((hid, width), BF16),
            pltpu.SemaphoreType.DMA((3,)),
        ],
        compiler_params=params(),
        cost_estimate=cost(6 * rows * width * hid, 11e6),
        name="item_own",
    )(cot, slope_up, slope_gate, w_gate, w_up, w_down)


def late_kernel(slots, before, scale, place_ref, *refs):
    count = len(slots)
    pieces, (column_hbm, normed_hbm, hidden_hbm, slope_up_hbm, slope_gate_hbm, down_hbm) = (
        refs[:count],
        refs[count : count + 6],
    )
    earlier, refs = (refs[count + 6 : count + 9], refs[count + 9 :]) if before else (None, refs[count + 6 :])
    outs, (cot, column, normed, hidden, slope_up, slope_gate, d_both, down, sems) = refs[:3], refs[3:]
    rows = cot.shape[0] // count
    block = column.shape[1]
    narrow = block % 128 != 0
    hid = hidden.shape[1]
    copies = [(piece, cot.at[pl.ds(k * rows, rows)]) for k, piece in enumerate(pieces)]
    copies += [(down_hbm.at[to], down.at[to]) for to in tiles(hid, TILE)]
    for k, slot in enumerate(slots):
        at, to = pl.ds(slot * rows, rows), pl.ds(k * rows, rows)
        copies += [(slope_up_hbm.at[at], slope_up.at[to]), (slope_gate_hbm.at[at], slope_gate.at[to])]
        copies += [(normed_hbm.at[at], normed.at[to]), (hidden_hbm.at[at], hidden.at[to])]
    if narrow:
        copies.append((column_hbm, column))
    loads = [pltpu.make_async_copy(src, dst, sems.at[k]) for k, (src, dst) in enumerate(copies)]
    for load in loads:
        load.start()
    for load in loads:
        load.wait()
    if not narrow:
        column[...] = cot[:, pl.ds(pl.multiple_of(place_ref[2] * block, 128), block)]
    for to in tiles(hid, TILE):
        d_hidden = mm(cot[...], down[to, :], LAST)
        d_both[:, to] = (d_hidden * slope_gate[:, to].astype(F32)).astype(BF16)
        at = slice(hid + to.start, hid + to.stop)
        d_both[:, at] = (d_hidden * slope_up[:, to].astype(F32)).astype(BF16)
    both_part = mm(normed[...], d_both[...], FIRST) * scale
    down_part = mm(column[...], hidden[...], FIRST).T * scale
    parts = (both_part[:, :hid], both_part[:, hid:], down_part)
    for k, part in enumerate(parts):
        outs[k][...] = (part + earlier[k][...].astype(F32) if before else part).astype(outs[k].dtype)


def item_late(
    place, slots, pieces, column, normed, hidden, slope_up, slope_gate, w_down, before, scale, kind
):
    count = len(pieces)
    rows, width = count * pieces[0].shape[0], pieces[0].shape[1]
    hid, block = w_down.shape[0], normed.shape[1]
    before = list(before) if before is not None else []
    return pl.pallas_call(
        functools.partial(late_kernel, tuple(slots), bool(before), scale),
        in_specs=[smem()] + [hbm()] * (count + 6) + [vmem()] * len(before),
        out_specs=[vmem()] * 3,
        out_shape=[
            jax.ShapeDtypeStruct((block, hid), kind),
            jax.ShapeDtypeStruct((block, hid), kind),
            jax.ShapeDtypeStruct((hid, block), kind),
        ],
        scratch_shapes=[
            pltpu.VMEM((rows, width), BF16),
            pltpu.VMEM((rows, block), BF16),
            pltpu.VMEM((rows, block), BF16),
            pltpu.VMEM((rows, hid), BF16),
            pltpu.VMEM((rows, hid), BF16),
            pltpu.VMEM((rows, hid), BF16),
            pltpu.VMEM((rows, 2 * hid), BF16),
            pltpu.VMEM((hid, width), BF16),
            pltpu.SemaphoreType.DMA((5 * count + 1 + len(tiles(hid, TILE)),)),
        ],
        compiler_params=params(),
        cost_estimate=cost(4 * rows * width * hid + 12 * rows * block * hid, 16e6),
        name="item_late",
    )(
        place, *pieces, column, normed, hidden, slope_up, slope_gate, w_down, *before,
    )


def merge_kernel(here_ref, kept_ref, got_ref, *refs):
    count = sum(1 for r in refs if r.shape == kept_ref.shape) - 1
    pieces, outs, total = refs[:count], refs[count:-1], refs[-1]
    value = kept_ref[...].astype(F32) + got_ref[...].astype(F32)
    for piece in pieces:
        value = value + piece[...].astype(F32)
    total[...] = value.astype(BF16)
    cut_rows(here_ref[0], total, outs)


def cut_rows(here, total, outs):
    rows = outs[0].shape[0]
    for k, out in enumerate(outs):
        out[...] = total[pl.ds(pl.multiple_of((here ^ k) * rows, rows), rows), :]


def merge_chips(here, kept, got, pieces, n_narrow):
    rows, width = pieces[0].shape
    spec = whole_spec((rows, width))
    part = (rows // n_narrow, width)
    return pl.pallas_call(
        merge_kernel,
        grid=(1,),
        in_specs=[smem()] + [spec] * (2 + len(pieces)),
        out_specs=[whole_spec(part)] * n_narrow,
        out_shape=[jax.ShapeDtypeStruct(part, BF16)] * n_narrow,
        scratch_shapes=[pltpu.VMEM((rows, width), BF16)],
        compiler_params=params(),
        cost_estimate=cost(0, 2 * (4 + len(pieces)) * rows * width),
        name="merge_chips",
    )(jnp.reshape(here, (1,)), kept, got, *pieces)


def final_kernel(scale, here_ref, kept_a, got_a, kept_b, got_b, *refs):
    slots, (feat_out, gate_out, up_out, down_out) = refs[:-4], refs[-4:]
    cut, hid = kept_a.shape[0], gate_out.shape[1]
    for half, (kept, got) in enumerate(((kept_a, got_a), (kept_b, got_b))):
        total = (kept[...].astype(F32) + got[...].astype(F32)) * scale
        at = slice(half * cut, (half + 1) * cut)
        gate_out[at, :] = total[:, :hid]
        up_out[at, :] = total[:, hid : 2 * hid]
        down_out[:, at] = total[:, 2 * hid :].T
    rows = slots[0].shape[0]
    for k, slot in enumerate(slots):
        feat_out[pl.ds(pl.multiple_of((here_ref[0] ^ k) * rows, rows), rows), :] = slot[...]


def final_sums(here, kept_a, got_a, kept_b, got_b, slots, scale):
    cut, hid = kept_a.shape[0], kept_a.shape[1] // 3
    rows, width = slots[0].shape
    return pl.pallas_call(
        functools.partial(final_kernel, scale),
        in_specs=[smem()] + [vmem()] * (4 + len(slots)),
        out_specs=[vmem()] * 4,
        out_shape=[
            jax.ShapeDtypeStruct((len(slots) * rows, width), BF16),
            jax.ShapeDtypeStruct((2 * cut, hid), F32),
            jax.ShapeDtypeStruct((2 * cut, hid), F32),
            jax.ShapeDtypeStruct((hid, 2 * cut), F32),
        ],
        compiler_params=params(),
        cost_estimate=cost(0, 30 * cut * hid),
        name="final_sums",
    )(jnp.reshape(here, (1,)), kept_a, got_a, kept_b, got_b, *slots)


def grad_tables(n_chips, order_a, order_b):
    first_a, first_b = order_a[0] >> 1, order_b[0] >> 1
    rels = sorted(range(n_chips), key=lambda r: (not (r & first_a), not (r & first_b), r))
    rows = [[], [], [], [], [], [], []]
    places = {}
    for name, first, row in (("a", first_a, 0), ("b", first_b, 3)):
        sent_order = [r for r in rels if r & first]
        kept_order = [r for r in rels if not r & first]
        last_sent = last_kept = 0
        for r in rels:
            is_sent = bool(r & first)
            if is_sent:
                last_sent = sent_order.index(r)
            else:
                last_kept = kept_order.index(r)
            rows[row].append(last_sent)
            rows[row + 1].append(last_kept)
            rows[row + 2].append(int(is_sent))
        places[name] = kept_order
    return np.array([rels, *rows[:6]], np.int32), places


def first_sums(got, kept, slots):
    return {r: (kept[i].astype(F32) + got[i].astype(F32)).astype(BF16) for i, r in enumerate(slots)}


def sent_away(total, bit):
    away = sorted(r for r in total if r & (bit >> 1))
    return jnp.stack([total[r] for r in away])


def next_sums(total, got, bit):
    away = sorted(r for r in total if r & (bit >> 1))
    return {
        r ^ (bit >> 1): (total[r ^ (bit >> 1)].astype(F32) + got[i].astype(F32)).astype(BF16)
        for i, r in enumerate(away)
    }


def body(
    user_input,
    out_grad,
    hist_len,
    hist_items,
    item_row,
    item_feat,
    user_gain,
    user_gate,
    user_up,
    user_down,
    item_gain,
    item_gate,
    item_up,
    item_down,
):
    n_wide, n_narrow = lax.axis_size("wide"), lax.axis_size("narrow")
    me, here = lax.axis_index("wide"), lax.axis_index("narrow")
    chip, core = me // 2, me % 2
    n_chips = n_wide // 2
    bits = [1 << k for k in range(1, n_wide.bit_length() - 1)]
    order_a = bits
    order_b = bits[len(bits) // 2 :] + bits[: len(bits) // 2]
    user_count, hist_length, width = user_input.shape
    rows = user_count * hist_length
    item_dev = item_feat.shape[0]
    hid = user_gate.shape[1]
    block = width // n_wide
    rels = jnp.arange(n_chips, dtype=jnp.int32)
    place = jnp.stack([chip, core, me, here])

    def near(value):
        return [value] + [swap(value, r << 1) for r in range(1, n_chips)]

    def gather_wide(value):
        pieces = near(value)
        return pieces + [swap(piece, 1) for piece in pieces]

    feats = gather_wide(item_feat)

    normed, masked, hidden, d_both, sent, kept = user_layer(
        place,
        hist_len,
        user_input.reshape(rows, width),
        out_grad.reshape(rows, width),
        hist_items,
        item_row,
        user_gain,
        user_gate,
        user_up,
        user_down,
        1.0 / n_narrow,
        item_dev,
    )
    sent, *_ = lax.optimization_barrier((sent, *feats[1:n_chips]))
    got = swap(sent, 1)
    grads_sent = sent_grads(place, (chip ^ rels) * 2 + 1 - core, normed, masked, d_both, hidden, block)
    got, grads_sent = lax.optimization_barrier((got, grads_sent))
    grads_got = swap(grads_sent, 1)
    sums = []
    for r in range(1, n_chips):
        at = slice(r * item_dev, (r + 1) * item_dev)
        sums.append((kept[at].astype(F32) + got[at].astype(F32)).astype(BF16))
    pieces = [swap(total, r << 1) for r, total in enumerate(sums, 1)]

    group = min(8, n_wide)
    forwards = [
        item_forward(place, item_gain, feats[k : k + group], item_gate, item_up, block, n_narrow)
        for k in range(0, n_wide, group)
    ]

    kept_table, places = grad_tables(n_chips, order_a, order_b)
    grads_got, _ = lax.optimization_barrier((grads_got, forwards[-1][0]))
    sent_a, kept_a, sent_b, kept_b = kept_grads(
        place, kept_table, (chip ^ jnp.asarray(kept_table[0])) * 2 + core,
        normed, masked, d_both, hidden, grads_got, block,
    )
    pieces[0], sent_a, sent_b = lax.optimization_barrier((pieces[0], sent_a, sent_b))
    mine = list(merge_chips(here, kept, got, pieces, n_narrow))
    sent_a, sent_b, mine[0] = lax.optimization_barrier((sent_a, sent_b, mine[0]))
    got_a, got_b = swap(sent_a, order_a[0]), swap(sent_b, order_b[0])

    quarter = item_dev // n_narrow

    def narrow_scatter(parts):
        got = [
            part if k == 0 else lax.ppermute(part, "narrow", [(i, i ^ k) for i in range(n_narrow)])
            for k, part in enumerate(parts)
        ]
        return functools.reduce(jnp.add, [part.astype(F32) for part in got])

    def narrow_slots(piece):
        return [piece] + [
            lax.ppermute(piece, "narrow", [(i, i ^ k) for i in range(n_narrow)])
            for k in range(1, n_narrow)
        ]

    item_in = narrow_scatter(mine)
    item_cot = jnp.concatenate(narrow_slots(item_in.astype(BF16)), axis=0)
    cots = [item_cot] + [swap(item_cot, r << 1) for r in range(1, n_chips - 1)]
    last_cot, *cots[1:] = lax.optimization_barrier((item_cot, *cots[1:]))
    cots.append(swap(last_cot, (n_chips - 1) << 1))
    item_part = item_own(
        item_cot, forwards[0][2], forwards[0][3], item_gate, item_up, item_down, n_narrow
    )
    item_dn = narrow_scatter(item_part)

    got_a, got_b, _ = lax.optimization_barrier((got_a, got_b, item_part[0]))
    assert len(order_a) > 1
    total_a = first_sums(got_a, kept_a, places["a"])
    total_b = first_sums(got_b, kept_b, places["b"])
    for a, b in zip(order_a[1:], order_b[1:]):
        away_a, away_b = sent_away(total_a, a), sent_away(total_b, b)
        away_a, away_b, cots[1] = lax.optimization_barrier((away_a, away_b, cots[1]))
        got_a, got_b = swap(away_a, a), swap(away_b, b)
        if a != order_a[-1]:
            total_a, total_b = next_sums(total_a, got_a, a), next_sums(total_b, got_b, b)
    cots = cots + [swap(piece, 1) for piece in cots]

    slots = range(n_wide)
    if n_wide == group:
        arrived = [k for k in slots if k % n_chips != n_chips - 1]
        lots = [arrived, [k for k in slots if k not in arrived]]
    else:
        lots = [list(slots[k : k + group]) for k in range(0, n_wide, group)]

    def late(lot, before):
        normed_k, hidden_k, slope_up_k, slope_gate_k = forwards[lot[0] // group]
        parts = [cots[k] for k in lot]
        column = parts[0]
        if block % 128:
            normed_k = lax.dynamic_slice_in_dim(normed_k, me * block, block, axis=1)
            column = jnp.concatenate(
                [lax.dynamic_slice_in_dim(p, me * block, block, axis=1) for p in parts], axis=0
            )
        return list(
            item_late(
                place, [k % group for k in lot], parts, column, normed_k, hidden_k, slope_up_k,
                slope_gate_k, item_down, before, 1.0 / n_wide,
                F32 if lot is lots[-1] or len(lots) > 2 else BF16,
            )
        )

    item_grads = late(lots[0], None)
    own_feat = lax.dynamic_slice_in_dim(item_feat, here * quarter, quarter, axis=0)
    own_feat, item_in, item_grads[0] = lax.optimization_barrier((own_feat, item_in, item_grads[0]))
    item_scaled = item_gain.astype(F32)[None, :] * item_dn
    own = own_feat.astype(F32)
    own_inv = lax.rsqrt(jnp.mean(own * own, axis=1, keepdims=True) + 1e-05)
    own_unit = own * own_inv
    item_mean = jnp.mean(item_scaled * own_unit, axis=1, keepdims=True)
    feat_rows = (item_in + own_inv * (item_scaled - own_unit * item_mean)).astype(BF16)
    feat_slots = narrow_slots(feat_rows)

    for lot in lots[1:]:
        item_grads = late(lot, item_grads)

    got_a, got_b, item_grads[0], *feat_slots = lax.optimization_barrier(
        (got_a, got_b, item_grads[0], *feat_slots)
    )
    feat_grad, *user_grads = final_sums(
        here, total_a[0], got_a[0], total_b[0], got_b[0], feat_slots, 1.0 / n_wide
    )
    return (feat_grad, *user_grads, *item_grads)


def solution(mesh):
    placed = (
        P("wide", None, None),
        P("wide", None, None),
        P("wide"),
        P("wide", None),
        P(),
        P("wide", None),
        P(),
        P(None, "narrow"),
        P(None, "narrow"),
        P("narrow", None),
        P(),
        P(None, "narrow"),
        P(None, "narrow"),
        P("narrow", None),
    )
    return jax.shard_map(
        body,
        mesh=mesh,
        in_specs=placed,
        out_specs=(
            P("wide", None),
            P("wide", "narrow"),
            P("wide", "narrow"),
            P("narrow", "wide"),
            P("wide", "narrow"),
            P("wide", "narrow"),
            P("narrow", "wide"),
        ),
        check_vma=False,
    )
```
